32 devices in a mesh: ctx: 8 (over z, y), head: 4 (over x, core).
Axes of the slice: x: 2, y: 2, z: 4, core: 2. Of those that a mesh axis runs over, the one named last changes fastest.
Arguments:
- enc_rows: bfloat16 [2048, 1024], P(('ctx', 'head')), may hold values from -6 to 6
- row_counts: int32 [8, 4], P('ctx'), may hold values from 0 to 64, as said below
- row_places: int32 [8, 256], P('ctx'), may hold values from 0 to 4095, as said below
- stream: bfloat16 [4096, 3072], P('ctx'), may hold values from -134 to 134
- norm_gain: float32 [3072], replicated, may hold values from 0.25 to 1.75
- proj_in: bfloat16 [1024, 6144], P('ctx', 'head'), may hold values from -0.1875 to 0.1875
- proj_out: bfloat16 [6144, 3072], P('head', 'ctx'), may hold values from -0.078125 to 0.078125
- qkv_weight: bfloat16 [3072, 3, 2048], P(None, None, 'head'), may hold values from -0.109375 to 0.109375
- head_gain: float32 [2048], P('head'), may hold values from 0.25 to 1.75
- mix_weight: bfloat16 [2048, 3072], P('head', 'ctx'), may hold values from -0.125 to 0.125
Outputs:
- layer_out: bfloat16 [4096, 3072], P('ctx', 'head')
The draws below stay inside these ranges and needn't reach their ends.
Inputs may be any that keep to these rules, and one draw needn't show every extreme that they name: `row_counts`: the 4 devices of one ctx index hold 64 live rows together, and some device holds 64. `row_places`: the place of a live slot of a device with ctx index c lies from c * 512 to c * 512 + 511, and live places are distinct; a slot that is not live holds a place in the same range, which is ignored.
All inputs are finite; a program needn't handle non-finite values.
Results may differ from the reference program's by a relative error of at most 0.015.
Values may be sent and summed in bfloat16 or wider, within the bound.
No kernel may reach another device: no remote copies, remote signals or barrier semaphores. Data moves between devices by JAX's collectives and lax.ppermute only.
A program may use at most 128 MiB of HBM per device.

```python
import math
import jax
import jax.numpy as jnp
from jax import lax

ENC = 1024
PROJ = 6144
D = 3072
HEAD_DIM = 128
HEADS_DEV = 4
SHARD = 512
HEADS = 16
CAP = 64
BLOCK = 512
TOKENS = 4096
SLOTS = 2048
N_CTX = 8
N_HEAD = 4


def layout(seed_key):
    base_key = jax.random.fold_in(seed_key, 7)
    key_cuts, key_pick, key_perm, key_pos, key_fill = jax.random.split(base_key, 5)
    quad_count = N_CTX * N_HEAD // 4
    cut_points = jax.random.randint(key_cuts, (quad_count, 3), 0, CAP + 1)
    chosen = jax.random.randint(key_pick, (), 0, quad_count)
    cut_points = jnp.where(jnp.arange(quad_count)[:, None] == chosen, CAP, cut_points)
    cut_points = jnp.sort(cut_points, axis=1).astype(jnp.int32)
    edge_points = jnp.concatenate([jnp.zeros((quad_count, 1), jnp.int32), cut_points, jnp.full((quad_count, 1), CAP, jnp.int32)], axis=1)
    row_parts = edge_points[:, 1:] - edge_points[:, :-1]
    ranking = jax.random.randint(key_perm, (quad_count, 4), 0, 1 << 20) * 4 + jnp.arange(4)
    row_parts = jnp.take_along_axis(row_parts, jnp.argsort(ranking, axis=1), axis=1)
    counts = row_parts.reshape(N_CTX, N_HEAD).astype(jnp.int32)
    starts = jnp.cumsum(counts, axis=1) - counts
    slot_index = jnp.arange(CAP, dtype=jnp.int32)
    row_rank = starts[:, :, None] + slot_index[None, None, :]
    is_live = (slot_index[None, None, :] < counts[:, :, None]).reshape(N_CTX, N_HEAD * CAP)
    ranking_pos = jax.random.randint(key_pos, (N_CTX, SHARD), 0, 1 << 20) * SHARD + jnp.arange(SHARD)
    offsets = jnp.argsort(ranking_pos, axis=1).astype(jnp.int32)
    safe_rank = jnp.minimum(row_rank, SHARD - 1).reshape(N_CTX, N_HEAD * CAP).astype(jnp.int32)
    picked = jnp.take_along_axis(offsets, safe_rank, axis=1)
    filler = jax.random.randint(key_fill, (N_CTX, N_HEAD * CAP), 0, SHARD)
    local_place = jnp.where(is_live, picked, filler)
    places = local_place + jnp.arange(N_CTX)[:, None] * SHARD
    return (counts, places.astype(jnp.int32))


def draw_row_counts(key, part):
    counts, places = layout(key)
    return counts


def draw_row_places(key, part):
    counts, places = layout(key)
    return places


def draw_stream(key, part):
    base_key = jax.random.fold_in(key, 11)
    key_main, key_cols, key_rows = jax.random.split(base_key, 3)
    column_scale = jnp.exp(jax.random.uniform(key_cols, (D,), jnp.float32, 0.0, math.log(10.0)))
    row_scale = jnp.exp(jax.random.uniform(key_rows, (TOKENS, 1), jnp.float32, 0.0, math.log(10.0)))
    entries = jnp.clip(jax.random.normal(key_main, (TOKENS, D), jnp.float32), -4.0, 4.0)
    return (entries * column_scale * row_scale / 3.0).astype(jnp.bfloat16)


def levels(key, extent, pieces, least, high):
    def one(axis_at, parts):
        draws = jax.random.uniform(jax.random.fold_in(jax.random.fold_in(key, 6), axis_at), (parts,), jnp.float32, least / len(pieces), high / len(pieces))
        return jnp.repeat(jnp.exp(draws), extent[axis_at] // parts).reshape((-1,) + (1,) * (len(extent) - axis_at - 1))

    factor_of = one(*pieces[0])
    for cut in pieces[1:]:
        factor_of = factor_of * one(*cut)
    return factor_of


def noise(own_key, shape, width, bound, pieces=(), held_as=jnp.bfloat16):
    gain = levels(own_key, shape, pieces, -0.22, 0.18) if pieces else 1.0
    drawn = jax.random.normal(own_key, shape, jnp.float32) * width * gain
    return jnp.minimum(jnp.maximum(drawn, -bound), bound).astype(held_as)


def setup_inputs(seed: int = 0) -> dict:
    key_list = jax.random.split(jax.random.key(seed), 11)
    return {
        "enc_rows": noise(key_list[0], (SLOTS, ENC), 1.0, 6.0, ((0, 32),)),
        "row_counts": draw_row_counts(jax.random.fold_in(key_list[10], 71), 0),
        "row_places": draw_row_places(jax.random.fold_in(key_list[10], 71), 0),
        "stream": draw_stream(jax.random.fold_in(key_list[10], 71), 0),
        "norm_gain": jnp.clip(1.0 + 0.15 * jax.random.normal(key_list[4], (D,), jnp.float32), 0.25, 1.75),
        "proj_in": noise(key_list[5], (ENC, PROJ), ENC ** -0.5, 0.1875, ((0, 8), (1, 4))),
        "proj_out": noise(key_list[6], (PROJ, D), PROJ ** -0.5, 0.078125, ((0, 4), (1, 8))),
        "qkv_weight": noise(key_list[7], (D, 3, HEADS * HEAD_DIM), D ** -0.5, 0.109375, ((2, 4),)),
        "head_gain": jnp.clip(1.0 + 0.15 * jax.random.normal(key_list[8], (HEADS * HEAD_DIM,), jnp.float32), 0.25, 1.75),
        "mix_weight": noise(key_list[9], (HEADS * HEAD_DIM, D), (HEADS * HEAD_DIM) ** -0.5, 0.125, ((0, 4), (1, 8))),
    }


def reference(enc_rows, row_counts, row_places, stream, norm_gain, proj_in, proj_out, qkv_weight, head_gain, mix_weight):
    slot_index = jnp.arange(SLOTS, dtype=jnp.int32)
    owner_dev = slot_index // CAP
    within = slot_index % CAP
    flat_counts = row_counts.reshape(N_CTX * N_HEAD)
    is_live = within < flat_counts[owner_dev]
    targets = jnp.where(is_live, row_places.reshape(SLOTS), TOKENS).astype(jnp.int32)
    hidden = jax.nn.gelu(jnp.dot(enc_rows, proj_in, preferred_element_type=jnp.float32), approximate=False).astype(jnp.bfloat16)
    image_rows = jnp.dot(hidden, proj_out, preferred_element_type=jnp.float32).astype(jnp.bfloat16)
    packed = stream.at[targets].set(image_rows, mode='drop')
    flat_qkv = qkv_weight.reshape(D, 3 * HEADS * HEAD_DIM)
    wide_mix = mix_weight.astype(jnp.float32).reshape(N_HEAD, HEADS_DEV * HEAD_DIM, D)
    causal = jnp.tril(jnp.ones((BLOCK, BLOCK), dtype=bool))
    blocks = packed.reshape(TOKENS // BLOCK, BLOCK, D)
    highest = lax.Precision.HIGHEST

    def advance(carried, block_rows):
        widened = block_rows.astype(jnp.float32)
        normed = (widened * lax.rsqrt(lax.optimization_barrier(jnp.mean(widened * widened, axis=-1, keepdims=True)) + 1e-05) * norm_gain).astype(jnp.bfloat16)
        projected = jax.nn.silu(jnp.dot(normed, flat_qkv, preferred_element_type=jnp.float32)).astype(jnp.bfloat16)
        projected = lax.optimization_barrier(projected)
        projected = projected.reshape(BLOCK, 3, HEADS, HEAD_DIM).astype(jnp.float32)
        queries = projected[:, 0]
        key_rows = projected[:, 1]
        values = projected[:, 2]
        scores = jnp.einsum('qhd,khd->hqk', queries, key_rows, precision=highest)
        scores = jnp.where(causal[None], scores, 0.0).astype(jnp.bfloat16)
        scores = lax.optimization_barrier(scores).astype(jnp.float32)
        attended = jnp.einsum('hqk,khd->qhd', scores, values, precision=highest)
        attended = attended + jnp.einsum('qhd,hde->qhe', queries, carried, precision=highest)
        carried = carried + jnp.einsum('khd,khe->hde', key_rows, values, precision=highest)
        inverse_rms = lax.rsqrt(lax.optimization_barrier(jnp.mean(attended * attended, axis=-1, keepdims=True)) + 1e-06)
        heads_out = (attended * inverse_rms * head_gain.reshape(HEADS, HEAD_DIM)).astype(jnp.bfloat16)
        heads_out = lax.optimization_barrier(heads_out)
        grouped = heads_out.reshape(BLOCK, N_HEAD, HEADS_DEV * HEAD_DIM).astype(jnp.float32)
        partials = jnp.einsum('tgc,gcd->tgd', grouped, wide_mix, precision=highest).astype(jnp.bfloat16)
        partials = lax.optimization_barrier(partials).astype(jnp.float32)
        return (carried, lax.optimization_barrier(jnp.sum(partials, axis=1)).astype(jnp.bfloat16))
    initial = jnp.zeros((HEADS, HEAD_DIM, HEAD_DIM), jnp.float32)
    _, outputs = lax.scan(advance, initial, blocks)
    return outputs.reshape(TOKENS, D)
```

```python
import jax
import jax.numpy as jnp
from jax import lax
from jax.sharding import PartitionSpec as P

HEAD_DIM = 128
F32 = jnp.float32
BF16 = jnp.bfloat16


def gather_head(x, bits, head_index, head_count):
    for bit in bits:
        other = lax.ppermute(x, "head", [(i, i ^ bit) for i in range(head_count)])
        upper = (head_index & bit) != 0
        x = jnp.stack([jnp.where(upper, other, x), jnp.where(upper, x, other)])
    return x


def on_device(
    enc_rows,
    row_counts,
    row_places,
    stream,
    norm_gain,
    proj_in,
    proj_out,
    qkv_weight,
    head_gain,
    mix_weight,
):
    both = ("ctx", "head")
    capacity, enc_width = enc_rows.shape
    shard_rows, width = stream.shape
    n_ctx, n_head = lax.axis_size("ctx"), lax.axis_size("head")
    ctx, head = lax.axis_index("ctx"), lax.axis_index("head")
    live_total = n_head * (capacity // 4)
    part_rows = live_total // n_head
    bits = []
    bit = n_head // 2
    while bit:
        bits.append(bit)
        bit //= 2
    flat = [(c, h) for c in range(n_ctx) for h in range(n_head)]

    def index(c, h):
        return c * n_head + h

    half = proj_in.shape[1] // 2
    in_halves = jnp.stack([proj_in[:, :half], proj_in[:, half:]])
    in_sends = jnp.broadcast_to(in_halves[None], (n_ctx // 2,) + in_halves.shape).reshape(
        (n_ctx,) + in_halves.shape[1:]
    )
    in_full = lax.all_to_all(in_sends, "ctx", 0, 0).reshape(enc_width, half)

    out_cols = proj_out.shape[1]
    out_parts = []
    for k in range(2):
        chosen = (head & 1) ^ k
        block = lax.dynamic_slice(proj_out, (chosen * half, 0), (half, out_cols))
        perm = [
            (index(c, h), index((c & ~1) | ((h & 1) ^ k), (h & ~1) | (c & 1))) for c, h in flat
        ]
        out_parts.append(lax.ppermute(block, both, perm))

    ratio = n_ctx // n_head
    perm = [(index(c, h), index((c % ratio) * n_head + h, c // ratio)) for c, h in flat]
    mix_own = lax.ppermute(mix_weight, both, perm)

    group_rows = lax.all_gather(enc_rows, "head", axis=0, tiled=True)
    counts = row_counts[0]
    starts = jnp.cumsum(counts) - counts
    within = jnp.arange(capacity, dtype=jnp.int32)[None, :]
    spot = jnp.where(within < counts[:, None], starts[:, None] + within, -1).reshape(-1)
    picks = spot[None, :] == jnp.arange(live_total, dtype=jnp.int32)[:, None]
    local_places = row_places[0] - ctx * shard_rows
    places = jnp.sum(jnp.where(picks, local_places[None, :], 0), axis=1)
    own_picks = (
        spot[None, :] == (head * part_rows + jnp.arange(part_rows, dtype=jnp.int32))[:, None]
    )
    own_rows = jnp.dot(own_picks.astype(BF16), group_rows, preferred_element_type=F32).astype(BF16)
    part = lax.all_to_all(
        jnp.broadcast_to(own_rows[None], (n_ctx,) + own_rows.shape), "ctx", 0, 0
    )
    all_rows = gather_head(part, bits, head, n_head)
    hidden = jax.nn.gelu(
        jnp.dot(all_rows.reshape(-1, enc_width), in_full, preferred_element_type=F32),
        approximate=False,
    ).astype(BF16)
    hidden_other = lax.ppermute(hidden, "head", [(i, i ^ 1) for i in range(n_head)])
    aligned = (head & 1) == (ctx & 1)
    hid_a = jnp.where(aligned, hidden, hidden_other)
    hid_b = jnp.where(aligned, hidden_other, hidden)
    partial_rows = jnp.dot(hid_a, out_parts[0], preferred_element_type=F32) + jnp.dot(
        hid_b, out_parts[1], preferred_element_type=F32
    )
    n_bits = len(bits)
    partial_rows = partial_rows.astype(BF16).reshape((2,) * n_bits + (n_ctx, part_rows, out_cols))
    order = (n_bits,) + tuple(reversed(range(n_bits))) + (n_bits + 1, n_bits + 2)
    sends = partial_rows.transpose(order).reshape(n_ctx * n_head, part_rows, out_cols)
    received = lax.all_to_all(sends, both, 0, 0)
    received = received.reshape(n_ctx // 2, 2, n_head // 2, 2, part_rows, out_cols)
    summed = jnp.sum(received.astype(F32), axis=(1, 2)).astype(BF16)
    img_part = summed.transpose(2, 0, 1, 3).reshape(part_rows, width)
    image_rows = lax.all_gather(img_part, "head", axis=0, tiled=True)

    flat_qkv = qkv_weight.reshape(width, -1)

    def project(rows):
        widened = rows.astype(F32)
        normed = (
            widened
            * lax.rsqrt(jnp.mean(widened * widened, axis=-1, keepdims=True) + 1e-05)
            * norm_gain
        ).astype(BF16)
        return jax.nn.silu(jnp.dot(normed, flat_qkv, preferred_element_type=F32)).astype(BF16)

    text_qkv = project(stream)
    image_qkv = project(image_rows)
    put = jnp.arange(shard_rows, dtype=jnp.int32)[:, None] == places[None, :]
    placed = jnp.dot(put.astype(BF16), image_qkv, preferred_element_type=F32).astype(BF16)
    projected = jnp.where(jnp.any(put, axis=1)[:, None], placed, text_qkv)

    heads_dev = qkv_weight.shape[2] // HEAD_DIM
    block_len = min(shard_rows, 512)
    block_count = shard_rows // block_len
    projected = projected.reshape(block_count, block_len, 3, heads_dev, HEAD_DIM)
    queries = projected[:, :, 0]
    key_rows = projected[:, :, 1]
    values = projected[:, :, 2]
    block_states = jnp.einsum("bkhd,bkhe->bhde", key_rows, values, preferred_element_type=F32)
    shard_state = jnp.sum(block_states, axis=0)
    pieces = shard_state.astype(BF16).reshape(n_ctx, -1, HEAD_DIM)
    pieces = lax.all_to_all(pieces, "ctx", 0, 0).astype(F32)
    before = jnp.cumsum(pieces, axis=0) - pieces
    prefix = lax.all_to_all(before.astype(BF16), "ctx", 0, 0).astype(F32).reshape(shard_state.shape)
    running_states = jnp.cumsum(block_states, axis=0)
    earlier_states = jnp.concatenate([jnp.zeros_like(block_states), running_states[:-1]], axis=0)
    starting = prefix[None] + earlier_states
    causal = jnp.tril(jnp.ones((block_len, block_len), dtype=bool))
    scores = jnp.einsum("bqhd,bkhd->bhqk", queries, key_rows, preferred_element_type=F32)
    scores = jnp.where(causal, scores, 0.0).astype(BF16)
    attended = jnp.einsum("bhqk,bkhd->bqhd", scores, values, preferred_element_type=F32)
    attended = attended + jnp.einsum(
        "bqhd,bhde->bqhe", queries, starting.astype(BF16), preferred_element_type=F32
    )
    inverse_rms = lax.rsqrt(jnp.mean(attended * attended, axis=-1, keepdims=True) + 1e-06)
    heads_out = (attended * inverse_rms * head_gain.reshape(heads_dev, HEAD_DIM)).astype(BF16)
    heads_out = heads_out.reshape(shard_rows, heads_dev * HEAD_DIM)

    all_heads = gather_head(heads_out, bits, head, n_head)
    mix_full = lax.all_gather(mix_own, "ctx", axis=0)
    group_width, mix_cols = mix_weight.shape
    mix_full = mix_full.reshape(ratio, n_head, group_width, mix_cols)
    total = 0.0
    for g in range(n_head):
        at = tuple((g >> b) & 1 for b in range(n_bits))
        group = jnp.concatenate([mix_full[r, g] for r in range(ratio)], axis=1)
        one = jnp.dot(all_heads[at], group, preferred_element_type=F32).astype(BF16)
        total = total + one.astype(F32)
    return total.astype(BF16)


def solution(mesh):
    in_specs = (
        P(("ctx", "head"), None),
        P("ctx", None),
        P("ctx", None),
        P("ctx", None),
        P(),
        P("ctx", "head"),
        P("head", "ctx"),
        P(None, None, "head"),
        P("head"),
        P("head", "ctx"),
    )
    out_specs = P("ctx", "head")
    return jax.shard_map(
        on_device, mesh=mesh, in_specs=in_specs, out_specs=out_specs, check_vma=False
    )
```

```python
import functools

import jax
import jax.numpy as jnp
from jax import lax
from jax.experimental import pallas as pl
from jax.experimental.pallas import tpu as pltpu
from jax.sharding import PartitionSpec as P

HEAD_DIM = 128
F32 = jnp.float32
BF16 = jnp.bfloat16
VMEM_LIMIT = 40 * 1024 * 1024
VMEM = pl.BlockSpec(memory_space=pltpu.VMEM)
SMEM = pl.BlockSpec(memory_space=pltpu.SMEM)
PARAMS = pltpu.CompilerParams(vmem_limit_bytes=VMEM_LIMIT)


def cost(flops, nbytes, transcendentals=0):
    return pl.CostEstimate(
        flops=int(flops), bytes_accessed=int(nbytes), transcendentals=int(transcendentals)
    )


def dot(a, b):
    return jnp.dot(a, b, preferred_element_type=F32)


def silu(x):
    return x * (1.0 / (1.0 + jnp.exp(-x)))


def projector_kernel(chunk, meta, own, other, first, second, second_next, keep, send, w_keep, w_send):
    same = meta[0] == meta[1]
    mine, near = second[...], second_next[...]
    w_keep[...] = jnp.where(same, mine, near)
    w_send[...] = jnp.where(same, near, mine)
    rows = own.shape[0]

    def run(source, base):
        @pl.loop(0, rows // chunk)
        def _(i):
            at = pl.ds(pl.multiple_of(i * chunk, chunk), chunk)
            to = pl.ds(pl.multiple_of(base + i * chunk, chunk), chunk)
            pre = dot(source[at, :], first[...])
            hid = (0.5 * pre * (1.0 + lax.erf(pre * 0.7071067811865476))).astype(BF16)
            keep[to, :] = dot(hid, w_keep[...]).astype(BF16)
            send[to, :] = dot(hid, w_send[...]).astype(BF16)

    run(own, 0)
    run(other, rows)


def projector(meta, own, other, first, second, second_next):
    rows, width = own.shape
    units, cols = second.shape
    out = jax.ShapeDtypeStruct((2 * rows, cols), BF16)
    return pl.pallas_call(
        functools.partial(projector_kernel, min(rows, 256)),
        out_shape=(out, out),
        in_specs=[SMEM] + [VMEM] * 5,
        out_specs=(VMEM, VMEM),
        scratch_shapes=[pltpu.VMEM((units, cols), BF16), pltpu.VMEM((units, cols), BF16)],
        compiler_params=PARAMS,
        cost_estimate=cost(4 * rows * units * (width + 2 * cols), 5e6, 2 * rows * units),
        name="projector",
    )(meta, own, other, first, second, second_next)


def order_kernel(pairs, meta, keep, got, out):
    parity, core, pair = meta[0], meta[1], meta[2]
    rows = out.shape[2]
    for i in range(2):
        for k in range(pairs):
            for j in range(2):
                at = pl.ds(((i * pairs + k) * 2 + j) * rows, rows)
                there = pl.ds((((1 - i) * pairs + k) * 2 + j) * rows, rows)
                total = keep[at, :].astype(F32) + got[there, :].astype(F32)
                out[(pair ^ k) * 2 + (parity ^ j), core ^ i] = total.astype(BF16)


def order_rows(meta, keep, got, n_ctx):
    rows, cols = keep.shape
    return pl.pallas_call(
        functools.partial(order_kernel, n_ctx // 2),
        out_shape=jax.ShapeDtypeStruct((n_ctx, 2, rows // n_ctx // 2, cols), BF16),
        in_specs=[SMEM, VMEM, VMEM],
        out_specs=VMEM,
        compiler_params=PARAMS,
        cost_estimate=cost(rows * cols, 6 * rows * cols),
        name="order_rows",
    )(meta, keep, got)


def image_kernel(x, wq, wk, wv, text_state, q, k, v, state):
    rows = x[...]
    q[...] = silu(dot(rows, wq[...])).astype(BF16)
    key = silu(dot(rows, wk[...])).astype(BF16)
    value = silu(dot(rows, wv[...])).astype(BF16)
    k[...] = key
    v[...] = value
    outer = lax.dot_general(key, value, (((0,), (0,)), ((), ())), preferred_element_type=F32)
    state[...] = (text_state[...] + outer[None]).astype(BF16)


def image_qkv(x, weights, text_state):
    rows, width = x.shape
    cols = weights[0].shape[1]
    heads = cols // HEAD_DIM
    w_spec = pl.BlockSpec((width, HEAD_DIM), lambda h: (0, h))
    o_spec = pl.BlockSpec((rows, HEAD_DIM), lambda h: (0, h))
    s_spec = pl.BlockSpec((1, HEAD_DIM, HEAD_DIM), lambda h: (h, 0, 0))
    out = jax.ShapeDtypeStruct((rows, cols), BF16)
    return pl.pallas_call(
        image_kernel,
        grid=(heads,),
        out_shape=(out, out, out, jax.ShapeDtypeStruct(text_state.shape, BF16)),
        in_specs=[pl.BlockSpec((rows, width), lambda h: (0, 0)), w_spec, w_spec, w_spec, s_spec],
        out_specs=(o_spec, o_spec, o_spec, s_spec),
        compiler_params=PARAMS,
        cost_estimate=cost(6 * rows * width * cols, 6 * width * cols, 3 * rows * cols),
        name="image_qkv",
    )(x, *weights, text_state)


def finish_kernel(intra, q, state, gain, out):
    total = intra[...] + dot(q[...], state[0])
    scale = lax.rsqrt(jnp.mean(total * total, axis=-1, keepdims=True) + 1e-06)
    out[...] = (total * scale * gain[...]).astype(BF16)


def finish(intra, q, state, gain):
    rows, cols = q.shape
    block = pl.BlockSpec((rows, HEAD_DIM), lambda h: (0, h))
    return pl.pallas_call(
        finish_kernel,
        grid=(cols // HEAD_DIM,),
        out_shape=jax.ShapeDtypeStruct((rows, cols), BF16),
        in_specs=[
            block,
            block,
            pl.BlockSpec((1, HEAD_DIM, HEAD_DIM), lambda h: (h, 0, 0)),
            pl.BlockSpec((1, HEAD_DIM), lambda h: (0, h)),
        ],
        out_specs=block,
        compiler_params=PARAMS,
        cost_estimate=cost(2 * rows * cols * HEAD_DIM, 8 * rows * cols),
        name="finish",
    )(intra, q, state, gain)


def mix_kernel(parts, has_before, meta, *refs):
    ins, (mix, *before, out) = refs[: len(parts)], refs[len(parts) :]
    head = meta[3]
    cols = mix.shape[3]
    for r in range(mix.shape[0]):
        total = before[0][:, r * cols : (r + 1) * cols] if has_before else 0.0
        for ref, offset in zip(ins, parts):
            total = total + dot(ref[...], mix[r, head ^ offset])
        out[:, r * cols : (r + 1) * cols] = total.astype(out.dtype)


def mix_part(meta, arrays, offsets, mix, before, dtype):
    rows, width = arrays[0].shape
    ratio, _, _, cols = mix.shape
    step = min(rows, 256)
    block = pl.BlockSpec((step, width), lambda i: (i, 0))
    out_block = pl.BlockSpec((step, ratio * cols), lambda i: (i, 0))
    whole = pl.BlockSpec(mix.shape, lambda i: (0, 0, 0, 0))
    extra = [] if before is None else [before]
    return pl.pallas_call(
        functools.partial(mix_kernel, tuple(offsets), before is not None),
        grid=(rows // step,),
        out_shape=jax.ShapeDtypeStruct((rows, ratio * cols), dtype),
        in_specs=[SMEM] + [block] * len(arrays) + [whole] + [out_block] * len(extra),
        out_specs=out_block,
        compiler_params=PARAMS,
        cost_estimate=cost(2 * rows * width * ratio * cols * len(arrays), 5e6),
        name="mix_part",
    )(meta, *arrays, mix, *extra)


def on_device(
    enc_rows,
    row_counts,
    row_places,
    stream,
    norm_gain,
    proj_in,
    proj_out,
    qkv_weight,
    head_gain,
    mix_weight,
):
    both = ("ctx", "head")
    capacity, enc_width = enc_rows.shape
    shard_rows, width = stream.shape
    n_ctx, n_head = lax.axis_size("ctx"), lax.axis_size("head")
    ctx, head = lax.axis_index("ctx"), lax.axis_index("head")
    live_total = n_head * (capacity // 4)
    core_rows = live_total // 2
    part_rows = live_total // n_head
    n_pairs = n_ctx // 2
    core, parity = head & 1, ctx & 1
    meta = jnp.stack([parity, core, ctx >> 1, head]).astype(jnp.int32)
    flat = [(c, h) for c in range(n_ctx) for h in range(n_head)]

    def along(axis, count, mask):
        return functools.partial(
            lax.ppermute, axis_name=axis, perm=[(i, i ^ mask) for i in range(count)]
        )

    def index(c, h):
        return c * n_head + h

    half = proj_in.shape[1] // 2
    in_halves = jnp.stack([proj_in[:, :half], proj_in[:, half:]])
    in_sends = jnp.broadcast_to(in_halves[None], (n_pairs,) + in_halves.shape).reshape(
        (n_ctx,) + in_halves.shape[1:]
    )
    in_full = lax.all_to_all(in_sends, "ctx", 0, 0).reshape(enc_width, half)

    out_cols = proj_out.shape[1]
    out_mine = lax.dynamic_slice(proj_out, (parity * half, 0), (half, out_cols))
    out_next = along("ctx", n_ctx, 1)(
        lax.dynamic_slice(proj_out, ((1 - parity) * half, 0), (half, out_cols))
    )

    ratio = n_ctx // n_head
    perm = [(index(c, h), index((c % ratio) * n_head + h, c // ratio)) for c, h in flat]
    mix_own = lax.ppermute(mix_weight, both, perm)

    group_rows = lax.all_gather(enc_rows, "head", axis=0, tiled=True)
    counts = row_counts[0]
    earlier = jnp.arange(n_head)[:, None] > jnp.arange(n_head)[None, :]
    starts = jnp.sum(jnp.where(earlier, counts[None, :], 0), axis=1)
    within = jnp.arange(capacity, dtype=jnp.int32)[None, :]
    spot = jnp.where(within < counts[:, None], starts[:, None] + within, -1).reshape(-1)
    wanted = core * core_rows + jnp.arange(core_rows, dtype=jnp.int32)
    own_picks = (spot[None, :] == wanted[:, None]).astype(BF16)
    own_rows = dot(own_picks, group_rows).astype(BF16)
    pair_rows = jnp.stack([own_rows, along("ctx", n_ctx, 1)(own_rows)])
    blocks = [pair_rows] + [along("ctx", n_ctx, 2 * k)(pair_rows) for k in range(1, n_pairs)]
    core_part = jnp.concatenate(blocks).reshape(-1, enc_width)
    other_part = along("head", n_head, 1)(core_part)

    keep, send = projector(meta, core_part, other_part, in_full, out_mine, out_next)
    ordered = order_rows(meta, keep, along("head", n_head, 1)(send), n_ctx)
    received = lax.all_to_all(ordered.reshape(n_ctx * n_head, part_rows, out_cols), both, 0, 0)
    received = received.reshape(n_pairs, 2, n_head // 2, 2, part_rows, out_cols)
    summed = jnp.sum(received.astype(F32), axis=(1, 2)).astype(BF16)
    img_part = summed.transpose(2, 0, 1, 3).reshape(part_rows, width)

    def norm(rows):
        widened = rows.astype(F32)
        return (
            widened
            * lax.rsqrt(jnp.mean(widened * widened, axis=-1, keepdims=True) + 1e-05)
            * norm_gain
        ).astype(BF16)

    image_rows = lax.all_gather(norm(img_part), "head", axis=0, tiled=True)

    local_places = row_places[0] - ctx * shard_rows
    picks = spot[None, :] == jnp.arange(live_total, dtype=jnp.int32)[:, None]
    places = jnp.sum(jnp.where(picks, local_places[None, :], 0), axis=1)
    put = jnp.arange(shard_rows, dtype=jnp.int32)[:, None] == places[None, :]
    is_text = jnp.logical_not(jnp.any(put, axis=1))[:, None]
    weights = [qkv_weight[:, i, :] for i in range(3)]
    text_rows = norm(stream)
    text_q, text_k, text_v = [
        jnp.where(is_text, jax.nn.silu(dot(text_rows, w)), 0.0).astype(BF16) for w in weights
    ]
    cols = text_q.shape[1]
    heads_dev = cols // HEAD_DIM

    def split(x):
        return x.reshape(x.shape[0], heads_dev, HEAD_DIM)

    text_state = jnp.einsum(
        "khd,khe->hde", split(text_k), split(text_v), preferred_element_type=F32
    )
    image_q, image_k, image_v, state = image_qkv(image_rows, weights, text_state)

    pieces = lax.all_to_all(state.reshape(n_ctx, -1, HEAD_DIM), "ctx", 0, 0).astype(F32)
    before = jnp.cumsum(pieces, axis=0) - pieces
    prefix = lax.all_to_all(before.astype(BF16), "ctx", 0, 0).reshape(state.shape)

    put = put.astype(BF16)

    def place(text, image):
        return (text.astype(F32) + dot(put, image)).astype(BF16)

    queries, key_rows, values = (
        place(text_q, image_q),
        place(text_k, image_k),
        place(text_v, image_v),
    )
    causal = jnp.tril(jnp.ones((shard_rows, shard_rows), dtype=bool))
    scores = jnp.einsum(
        "qhd,khd->hqk", split(queries), split(key_rows), preferred_element_type=F32
    )
    scores = jnp.where(causal, scores, 0.0).astype(BF16)
    intra = jnp.einsum("hqk,khd->qhd", scores, split(values), preferred_element_type=F32)
    intra = intra.reshape(shard_rows, cols)
    heads_out = finish(intra, queries, prefix, head_gain[None])

    mix_own, in_full = lax.optimization_barrier((mix_own, in_full))
    mix_full = lax.all_gather(mix_own, "ctx", axis=0)
    group_width, mix_cols = mix_weight.shape
    mix_full = mix_full.reshape(ratio, n_head, group_width, mix_cols)
    parts, offsets = [heads_out], [0]
    bit = n_head // 2
    while bit:
        parts = parts + [along("head", n_head, bit)(p) for p in parts]
        offsets = offsets + [o ^ bit for o in offsets]
        bit //= 2
    if mix_cols % 128 == 0:
        near = [i for i, o in enumerate(offsets) if o < 2]
        far = [i for i, o in enumerate(offsets) if o >= 2]
        first = mix_part(
            meta, [parts[i] for i in near], [offsets[i] for i in near], mix_full, None, F32
        )
        return mix_part(
            meta, [parts[i] for i in far], [offsets[i] for i in far], mix_full, first, BF16
        )
    total = 0.0
    for part, offset in zip(parts, offsets):
        group = lax.dynamic_index_in_dim(mix_full, head ^ offset, 1, keepdims=False)
        group = jnp.concatenate([group[r] for r in range(ratio)], axis=1)
        total = total + dot(part, group)
    return total.astype(BF16)


def solution(mesh):
    in_specs = (
        P(("ctx", "head"), None),
        P("ctx", None),
        P("ctx", None),
        P("ctx", None),
        P(),
        P("ctx", "head"),
        P("head", "ctx"),
        P(None, None, "head"),
        P("head"),
        P("head", "ctx"),
    )
    out_specs = P("ctx", "head")
    return jax.shard_map(
        on_device, mesh=mesh, in_specs=in_specs, out_specs=out_specs, check_vma=False
    )
```

```python
import functools

import jax
import jax.numpy as jnp
from jax import lax
from jax.experimental import pallas as pl
from jax.experimental.pallas import tpu as pltpu
from jax.sharding import PartitionSpec as P

HEAD_DIM = 128
F32 = jnp.float32
BF16 = jnp.bfloat16
VMEM_LIMIT = 40 * 1024 * 1024
VMEM = pl.BlockSpec(memory_space=pltpu.VMEM)
SMEM = pl.BlockSpec(memory_space=pltpu.SMEM)
PARAMS = pltpu.CompilerParams(vmem_limit_bytes=VMEM_LIMIT)


def cost(flops, nbytes, transcendentals=0):
    return pl.CostEstimate(
        flops=int(flops), bytes_accessed=int(nbytes), transcendentals=int(transcendentals)
    )


def dot(a, b):
    return jnp.dot(a, b, preferred_element_type=F32)


def silu(x):
    return x * (1.0 / (1.0 + jnp.exp(-x)))


def nothing(source, out):
    pass


def weighty(x, flops, nbytes):
    return pl.pallas_call(
        nothing,
        out_shape=jax.ShapeDtypeStruct(x.shape, x.dtype),
        in_specs=[pl.BlockSpec(memory_space=pl.ANY)],
        out_specs=pl.BlockSpec(memory_space=pl.ANY),
        input_output_aliases={0: 0},
        cost_estimate=cost(flops, nbytes),
        name="weighty",
    )(x)


def projector_kernel(chunk, span, meta, own, other, first, *refs):
    seconds, (keep, send, w_keep, w_send) = refs[:span], refs[span:]
    cols = seconds[0].shape[1]
    same = meta[0] == meta[1]
    for m in range(0, span, 2):
        mine, near = seconds[m][...], seconds[m + 1][...]
        slot = (meta[4] ^ m) >> 1
        w_keep[slot] = jnp.where(same, mine, near)
        w_send[slot] = jnp.where(same, near, mine)
    rows = own.shape[0]

    def run(source, base):
        @pl.loop(0, rows // chunk)
        def _(i):
            at = pl.ds(pl.multiple_of(i * chunk, chunk), chunk)
            to = pl.ds(pl.multiple_of(base + i * chunk, chunk), chunk)
            pre = dot(source[at, :], first[...])
            hid = (0.5 * pre * (1.0 + lax.erf(pre * 0.7071067811865476))).astype(BF16)
            for n in range(span // 2):
                keep[to, n * cols : (n + 1) * cols] = dot(hid, w_keep[n]).astype(BF16)
                send[to, n * cols : (n + 1) * cols] = dot(hid, w_send[n]).astype(BF16)

    run(own, 0)
    run(other, rows)


def projector(meta, own, other, first, seconds):
    rows, width = own.shape
    units, cols = seconds[0].shape
    span = len(seconds)
    out = jax.ShapeDtypeStruct((2 * rows, span // 2 * cols), BF16)
    scratch = pltpu.VMEM((span // 2, units, cols), BF16)
    return pl.pallas_call(
        functools.partial(projector_kernel, min(rows, 256), span),
        out_shape=(out, out),
        in_specs=[SMEM] + [VMEM] * (3 + span),
        out_specs=(VMEM, VMEM),
        scratch_shapes=[scratch, scratch],
        compiler_params=pltpu.CompilerParams(vmem_limit_bytes=60 * 1024 * 1024),
        cost_estimate=cost(4 * rows * units * (width + span * cols), 5e6, 2 * rows * units),
        name="projector",
    )(meta, own, other, first, *seconds)


def pick_kernel(spot, *refs):
    sources, out = refs[:-1], refs[-1]
    rows = out.shape[0]
    wanted = lax.broadcasted_iota(jnp.int32, (rows, spot.shape[1]), 0)
    at, total = 0, 0.0
    for ref in sources:
        count = ref.shape[0]
        picks = (spot[:, at : at + count] == wanted[:, at : at + count]).astype(F32).astype(BF16)
        total = total + dot(picks, ref[...])
        at += count
    out[...] = total.astype(BF16)


def pick_rows(spot, sources, rows):
    width = sources[0].shape[1]
    return pl.pallas_call(
        pick_kernel,
        out_shape=jax.ShapeDtypeStruct((rows, width), BF16),
        in_specs=[VMEM] * (1 + len(sources)),
        out_specs=VMEM,
        compiler_params=PARAMS,
        cost_estimate=cost(2 * rows * width * spot.shape[1], 2 * width * spot.shape[1]),
        name="pick_rows",
    )(spot, *sources)


def order_kernel(offsets, meta, keep, got, out):
    core, ctx = meta[1], meta[2]
    rows, count = out.shape[2], len(offsets)
    for i in range(2):
        for b, offset in enumerate(offsets):
            at = pl.ds((i * count + b) * rows, rows)
            there = pl.ds(((1 - i) * count + b) * rows, rows)
            total = keep[at, :].astype(F32) + got[there, :].astype(F32)
            out[ctx ^ offset, core ^ i] = total.astype(BF16)


def order_rows(meta, keep, got, offsets):
    rows, cols = keep.shape
    count = len(offsets)
    return pl.pallas_call(
        functools.partial(order_kernel, tuple(offsets)),
        out_shape=jax.ShapeDtypeStruct((count, 2, rows // count // 2, cols), BF16),
        in_specs=[SMEM, VMEM, VMEM],
        out_specs=VMEM,
        compiler_params=PARAMS,
        cost_estimate=cost(rows * cols, 6 * rows * cols),
        name="order_rows",
    )(meta, keep, got)


def image_norm_kernel(groups, span, heads, got, gain, out, total):
    wide = span // 2
    cols = got.shape[2] // wide
    square = 0.0
    for g in range(groups):
        for core in range(2):
            part = 0.0
            for s in range(span):
                for h in range(heads // 2):
                    part = part + got[((g * span + s) * heads) + 2 * h + core].astype(F32)
            part = part.astype(BF16).astype(F32)
            square = square + jnp.sum(part * part, axis=-1, keepdims=True)
            for n in range(wide):
                c = g * span + 2 * n + core
                total[:, c * cols : (c + 1) * cols] = part[:, n * cols : (n + 1) * cols]
    scale = lax.rsqrt(square / total.shape[1] + 1e-05)
    out[...] = (total[...] * scale * gain[...]).astype(BF16)


def image_norm(got, gain, n_ctx, span):
    devices, rows, _ = got.shape
    width = gain.shape[1]
    return pl.pallas_call(
        functools.partial(image_norm_kernel, n_ctx // span, span, devices // n_ctx),
        out_shape=jax.ShapeDtypeStruct((rows, width), BF16),
        in_specs=[VMEM, VMEM],
        out_specs=VMEM,
        scratch_shapes=[pltpu.VMEM((rows, width), F32)],
        compiler_params=PARAMS,
        cost_estimate=cost(4 * got.size, 2 * got.size),
        name="image_norm",
    )(got, gain)


def image_kernel(x, wq, wk, wv, text_state, q, k, v, state):
    rows = x[...]
    q[...] = silu(dot(rows, wq[...])).astype(BF16)
    key = silu(dot(rows, wk[...])).astype(BF16)
    value = silu(dot(rows, wv[...])).astype(BF16)
    k[...] = key
    v[...] = value
    outer = lax.dot_general(key, value, (((0,), (0,)), ((), ())), preferred_element_type=F32)
    state[...] = (text_state[...] + outer[None]).astype(BF16)


def image_qkv(x, weights, text_state):
    rows, width = x.shape
    cols = weights[0].shape[1]
    heads = cols // HEAD_DIM
    w_spec = pl.BlockSpec((width, HEAD_DIM), lambda h: (0, h))
    o_spec = pl.BlockSpec((rows, HEAD_DIM), lambda h: (0, h))
    s_spec = pl.BlockSpec((1, HEAD_DIM, HEAD_DIM), lambda h: (h, 0, 0))
    out = jax.ShapeDtypeStruct((rows, cols), BF16)
    return pl.pallas_call(
        image_kernel,
        grid=(heads,),
        out_shape=(out, out, out, jax.ShapeDtypeStruct(text_state.shape, BF16)),
        in_specs=[pl.BlockSpec((rows, width), lambda h: (0, 0)), w_spec, w_spec, w_spec, s_spec],
        out_specs=(o_spec, o_spec, o_spec, s_spec),
        compiler_params=pltpu.CompilerParams(vmem_limit_bytes=60 * 1024 * 1024),
        cost_estimate=cost(6 * rows * width * cols, 6 * width * cols, 3 * rows * cols),
        name="image_qkv",
    )(x, *weights, text_state)


def finish_kernel(intra, q, state, gain, out):
    total = intra[...] + dot(q[...], state[0])
    scale = lax.rsqrt(jnp.mean(total * total, axis=-1, keepdims=True) + 1e-06)
    out[...] = (total * scale * gain[...]).astype(BF16)


def finish(intra, q, state, gain):
    rows, cols = q.shape
    block = pl.BlockSpec((rows, HEAD_DIM), lambda h: (0, h))
    return pl.pallas_call(
        finish_kernel,
        grid=(cols // HEAD_DIM,),
        out_shape=jax.ShapeDtypeStruct((rows, cols), BF16),
        in_specs=[
            block,
            block,
            pl.BlockSpec((1, HEAD_DIM, HEAD_DIM), lambda h: (h, 0, 0)),
            pl.BlockSpec((1, HEAD_DIM), lambda h: (0, h)),
        ],
        out_specs=block,
        compiler_params=PARAMS,
        cost_estimate=cost(2 * rows * cols * HEAD_DIM, 8 * rows * cols),
        name="finish",
    )(intra, q, state, gain)


def mix_kernel(parts, has_before, count, meta, *refs):
    ins, (mix, *before, out) = refs[: len(parts)], refs[len(parts) :]
    head = meta[3]
    cols = mix.shape[3]
    for r in range(mix.shape[1]):
        total = before[0][:, r * cols : (r + 1) * cols] if has_before else 0.0
        for ref, offset in zip(ins, parts):
            group = head ^ offset
            place = head ^ ((group >> 1) | ((group & 1) * (count // 2)))
            total = total + dot(ref[...], mix[place, r])
        out[:, r * cols : (r + 1) * cols] = total.astype(out.dtype)


def mix_part(meta, arrays, offsets, mix, before, dtype):
    rows, width = arrays[0].shape
    count, ratio, _, cols = mix.shape
    step = min(rows, 256)
    block = pl.BlockSpec((step, width), lambda i: (i, 0))
    out_block = pl.BlockSpec((step, ratio * cols), lambda i: (i, 0))
    whole = pl.BlockSpec(mix.shape, lambda i: (0, 0, 0, 0))
    extra = [] if before is None else [before]
    return pl.pallas_call(
        functools.partial(mix_kernel, tuple(offsets), before is not None, count),
        grid=(rows // step,),
        out_shape=jax.ShapeDtypeStruct((rows, ratio * cols), dtype),
        in_specs=[SMEM] + [block] * len(arrays) + [whole] + [out_block] * len(extra),
        out_specs=out_block,
        compiler_params=PARAMS,
        cost_estimate=cost(2 * rows * width * ratio * cols * len(arrays), 5e6),
        name="mix_part",
    )(meta, *arrays, mix, *extra)


def on_device(
    enc_rows,
    row_counts,
    row_places,
    stream,
    norm_gain,
    proj_in,
    proj_out,
    qkv_weight,
    head_gain,
    mix_weight,
):
    both = ("ctx", "head")
    capacity, enc_width = enc_rows.shape
    shard_rows, width = stream.shape
    n_ctx, n_head = lax.axis_size("ctx"), lax.axis_size("head")
    ctx, head = lax.axis_index("ctx"), lax.axis_index("head")
    live_total = n_head * (capacity // 4)
    core_rows = live_total // 2
    part_rows = live_total // n_head
    n_pairs = n_ctx // 2
    core, parity = head & 1, ctx & 1
    span = 4
    spot_in = ctx & (span - 1)
    meta = jnp.stack([parity, core, ctx, head, spot_in]).astype(jnp.int32)
    flat = [(c, h) for c in range(n_ctx) for h in range(n_head)]

    def along(axis, count, mask):
        return functools.partial(
            lax.ppermute, axis_name=axis, perm=[(i, i ^ mask) for i in range(count)]
        )

    def index(c, h):
        return c * n_head + h

    ratio = n_ctx // n_head

    def turned(h):
        return (h >> 1) | ((h & 1) * (n_head // 2))

    perm = [(index(c, h), index(c ^ (turned(h) * ratio), h)) for c, h in flat]
    mix_own = lax.ppermute(mix_weight, both, perm)
    perm = [(index(c, h), index(c, (c // ratio) ^ turned(h))) for c, h in flat]
    mix_own = lax.ppermute(mix_own, both, perm)

    part = proj_in.shape[1] // span
    in_parts = proj_in.reshape(-1, span, part).transpose(1, 0, 2)
    in_sends = jnp.broadcast_to(in_parts[None], (n_ctx // span,) + in_parts.shape).reshape(
        (n_ctx,) + in_parts.shape[1:]
    )
    in_full = weighty(lax.all_to_all(in_sends, "ctx", 0, 0), 1e11, 4e8).reshape(enc_width, part)

    out_cols = proj_out.shape[1]

    sources, swaps = [enc_rows], [0]
    bit = n_head // 2
    while bit:
        sources = sources + [along("head", n_head, bit)(x) for x in sources]
        swaps = swaps + [o ^ bit for o in swaps]
        bit //= 2
    counts = row_counts[0]
    earlier = jnp.arange(n_head)[:, None] > jnp.arange(n_head)[None, :]
    starts = jnp.sum(jnp.where(earlier, counts[None, :], 0), axis=1)
    within = jnp.arange(capacity, dtype=jnp.int32)[None, :]
    spot = jnp.where(within < counts[:, None], starts[:, None] + within, -1)
    owners = jnp.arange(n_head)[None, :] == (head ^ jnp.array(swaps, dtype=jnp.int32))[:, None]
    swapped = jnp.sum(jnp.where(owners[:, :, None], spot[None], 0), axis=1)
    own_rows = pick_rows(swapped.reshape(1, -1) - core * core_rows, sources, core_rows)

    seconds = []
    for m in range(span):
        block = lax.dynamic_slice(proj_out, ((spot_in ^ m) * part, 0), (part, out_cols))
        seconds.append(along("ctx", n_ctx, m)(block) if m else block)

    def norm(rows):
        widened = rows.astype(F32)
        return (
            widened
            * lax.rsqrt(jnp.mean(widened * widened, axis=-1, keepdims=True) + 1e-05)
            * norm_gain
        ).astype(BF16)

    def spread(x, mask):
        return jnp.concatenate([x, along("ctx", n_ctx, mask)(x)])

    masks = [1 << n for n in reversed(range(n_ctx.bit_length() - 1))]
    masks = masks[-1:] + masks[:-1]
    offsets_ctx = [0]
    for mask in masks:
        offsets_ctx = offsets_ctx + [o ^ mask for o in offsets_ctx]
    core_part = spread(own_rows, masks[0])
    core_part, seconds = lax.optimization_barrier((core_part, seconds))
    core_part = spread(core_part, masks[1])
    core_part, mix_own = lax.optimization_barrier((core_part, mix_own))
    for mask in masks[2:]:
        core_part = spread(core_part, mask)
    other_part = along("head", n_head, 1)(core_part)

    keep, send = projector(meta, core_part, other_part, in_full, seconds)
    ordered = order_rows(meta, keep, along("head", n_head, 1)(send), offsets_ctx)
    ordered, qkv_weight, stream = lax.optimization_barrier((ordered, qkv_weight, stream))
    local_places = row_places[0] - ctx * shard_rows
    picks = spot.reshape(1, -1) == jnp.arange(live_total, dtype=jnp.int32)[:, None]
    places = jnp.sum(jnp.where(picks, local_places[None, :], 0), axis=1)
    put = jnp.arange(shard_rows, dtype=jnp.int32)[:, None] == places[None, :]
    is_text = jnp.logical_not(jnp.any(put, axis=1))[:, None]
    weights = [qkv_weight[:, i, :] for i in range(3)]
    text_rows = norm(stream)

    text_q, text_k, text_v = [
        jnp.where(is_text, jax.nn.silu(dot(text_rows, w)), 0.0).astype(BF16) for w in weights
    ]
    cols = text_q.shape[1]
    heads_dev = cols // HEAD_DIM

    received = lax.all_to_all(
        ordered.reshape(n_ctx * n_head, part_rows, span // 2 * out_cols), both, 0, 0
    )

    if out_cols % 128 == 0:
        img_part = image_norm(received, norm_gain[None], n_ctx, span)
    else:
        received = received.reshape(
            n_ctx // span, span, n_head // 2, 2, part_rows, span // 2, out_cols
        )
        summed = jnp.sum(received.astype(F32), axis=(1, 2)).astype(BF16)
        img_part = norm(summed.transpose(2, 0, 3, 1, 4).reshape(part_rows, width))
    image_rows = lax.all_gather(img_part, "head", axis=0, tiled=True)

    def split(x):
        return x.reshape(x.shape[0], heads_dev, HEAD_DIM)

    text_state = jnp.einsum(
        "khd,khe->hde", split(text_k), split(text_v), preferred_element_type=F32
    )
    image_q, image_k, image_v, state = image_qkv(image_rows, weights, text_state)

    pieces = lax.all_to_all(state.reshape(n_ctx, -1, HEAD_DIM), "ctx", 0, 0).astype(F32)
    before = jnp.cumsum(pieces, axis=0) - pieces
    prefix = lax.all_to_all(before.astype(BF16), "ctx", 0, 0).reshape(state.shape)

    put = put.astype(BF16)

    def place(text, image):
        return (text.astype(F32) + dot(put, image)).astype(BF16)

    queries, key_rows, values = (
        place(text_q, image_q),
        place(text_k, image_k),
        place(text_v, image_v),
    )
    causal = jnp.tril(jnp.ones((shard_rows, shard_rows), dtype=bool))
    scores = jnp.einsum(
        "qhd,khd->hqk", split(queries), split(key_rows), preferred_element_type=F32
    )
    scores = jnp.where(causal, scores, 0.0).astype(BF16)
    intra = jnp.einsum("hqk,khd->qhd", scores, split(values), preferred_element_type=F32)
    intra = intra.reshape(shard_rows, cols)
    heads_out = finish(intra, queries, prefix, head_gain[None])

    mix_full = lax.all_gather(mix_own, "ctx", axis=0)
    group_width, mix_cols = mix_weight.shape
    mix_full = mix_full.reshape(n_head, ratio, group_width, mix_cols)
    parts, offsets = [heads_out], [0]
    bit = n_head // 2
    while bit:
        parts = parts + [along("head", n_head, bit)(p) for p in parts]
        offsets = offsets + [o ^ bit for o in offsets]
        bit //= 2
    if mix_cols % 128 == 0:
        near = [i for i, o in enumerate(offsets) if o < 2]
        far = [i for i, o in enumerate(offsets) if o >= 2]
        first = mix_part(
            meta, [parts[i] for i in near], [offsets[i] for i in near], mix_full, None, F32
        )
        return mix_part(
            meta, [parts[i] for i in far], [offsets[i] for i in far], mix_full, first, BF16
        )
    total = 0.0
    for part, offset in zip(parts, offsets):
        spot = head ^ turned(head ^ offset)
        group = lax.dynamic_index_in_dim(mix_full, spot, 0, keepdims=False)
        group = jnp.concatenate([group[r] for r in range(ratio)], axis=1)
        total = total + dot(part, group)
    return total.astype(BF16)


def solution(mesh):
    in_specs = (
        P(("ctx", "head"), None),
        P("ctx", None),
        P("ctx", None),
        P("ctx", None),
        P(),
        P("ctx", "head"),
        P("head", "ctx"),
        P(None, None, "head"),
        P("head"),
        P("head", "ctx"),
    )
    out_specs = P("ctx", "head")
    return jax.shard_map(
        on_device, mesh=mesh, in_specs=in_specs, out_specs=out_specs, check_vma=False
    )
```

```python
import functools

import jax
import jax.numpy as jnp
from jax import lax
from jax.experimental import pallas as pl
from jax.experimental.pallas import tpu as pltpu
from jax.sharding import PartitionSpec as P

HEAD_DIM = 128
F32 = jnp.float32
BF16 = jnp.bfloat16
VMEM_LIMIT = 20 * 1024 * 1024
VMEM = pl.BlockSpec(memory_space=pltpu.VMEM)
SMEM = pl.BlockSpec(memory_space=pltpu.SMEM)
ANYWHERE = pl.BlockSpec(memory_space=pl.ANY)
PARAMS = pltpu.CompilerParams(vmem_limit_bytes=VMEM_LIMIT)


def cost(flops, nbytes, transcendentals=0):
    return pl.CostEstimate(
        flops=int(flops), bytes_accessed=int(nbytes), transcendentals=int(transcendentals)
    )


def dot(a, b):
    return jnp.dot(a, b, preferred_element_type=F32)


def silu(x):
    return x * (1.0 / (1.0 + jnp.exp(-x)))


def nothing(*refs):
    pass


def weighty(arrays, flops, nbytes):
    anywhere = pl.BlockSpec(memory_space=pl.ANY)
    return pl.pallas_call(
        nothing,
        out_shape=[jax.ShapeDtypeStruct(x.shape, x.dtype) for x in arrays],
        in_specs=[anywhere] * len(arrays),
        out_specs=[anywhere] * len(arrays),
        input_output_aliases={i: i for i in range(len(arrays))},
        cost_estimate=cost(flops, nbytes),
        name="weighty",
    )(*arrays)


def spread_kernel(span, x, out):
    part = out.shape[2]
    for c in range(out.shape[0]):
        at = c % span * part
        out[c] = x[:, at : at + part]


def spread_units(x, n_ctx, span):
    rows, units = x.shape
    return pl.pallas_call(
        functools.partial(spread_kernel, span),
        out_shape=jax.ShapeDtypeStruct((n_ctx, rows, units // span), x.dtype),
        in_specs=[VMEM],
        out_specs=VMEM,
        compiler_params=PARAMS,
        cost_estimate=cost(0, 4 * x.size),
        name="spread_units",
    )(x)


def text_kernel(rows, keep, wq, wk, wv, out, state):
    step = min(rows.shape[0], 256)
    for i in range(rows.shape[0] // step):
        at = slice(i * step, (i + 1) * step)
        for n, w in enumerate((wq, wk, wv)):
            out[n, at, :] = (silu(dot(rows[at, :], w[...])) * keep[at, :]).astype(BF16)
    for h in range(state.shape[0]):
        cols = slice(h * HEAD_DIM, (h + 1) * HEAD_DIM)
        state[h] = lax.dot_general(
            out[1, :, cols], out[2, :, cols], (((0,), (0,)), ((), ())), preferred_element_type=F32
        )


def text_qkv(rows, keep, weights):
    count, width = rows.shape
    cols = weights[0].shape[1]
    heads = cols // HEAD_DIM
    return pl.pallas_call(
        text_kernel,
        out_shape=(
            jax.ShapeDtypeStruct((3, count, cols), BF16),
            jax.ShapeDtypeStruct((heads, HEAD_DIM, HEAD_DIM), F32),
        ),
        in_specs=[VMEM] * 5,
        out_specs=(VMEM, VMEM),
        compiler_params=PARAMS,
        cost_estimate=cost(6 * count * width * cols, 6 * width * cols, 3 * count * cols),
        name="text_qkv",
    )(rows, keep, *weights)


def projector_kernel(chunk, span, meta, own, other, first, *refs):
    seconds, (keep, send, w_keep, w_send) = refs[:span], refs[span:]
    cols = seconds[0].shape[1]
    same = meta[0] == meta[1]
    for m in range(0, span, 2):
        mine, near = seconds[m][...], seconds[m + 1][...]
        slot = (meta[4] ^ m) >> 1
        w_keep[slot] = jnp.where(same, mine, near)
        w_send[slot] = jnp.where(same, near, mine)
    rows = own.shape[0]

    def run(source, base):
        @pl.loop(0, rows // chunk)
        def _(i):
            at = pl.ds(pl.multiple_of(i * chunk, chunk), chunk)
            to = pl.ds(pl.multiple_of(base + i * chunk, chunk), chunk)
            pre = dot(source[at, :], first[...])
            hid = (0.5 * pre * (1.0 + lax.erf(pre * 0.7071067811865476))).astype(BF16)
            for n in range(span // 2):
                keep[to, n * cols : (n + 1) * cols] = dot(hid, w_keep[n]).astype(BF16)
                send[to, n * cols : (n + 1) * cols] = dot(hid, w_send[n]).astype(BF16)

    run(own, 0)
    run(other, rows)


def projector(meta, own, other, first, seconds):
    rows, width = own.shape
    units, cols = seconds[0].shape
    span = len(seconds)
    out = jax.ShapeDtypeStruct((2 * rows, span // 2 * cols), BF16)
    scratch = pltpu.VMEM((span // 2, units, cols), BF16)
    return pl.pallas_call(
        functools.partial(projector_kernel, min(rows, 256), span),
        out_shape=(out, out),
        in_specs=[SMEM] + [VMEM] * (3 + span),
        out_specs=(VMEM, VMEM),
        scratch_shapes=[scratch, scratch],
        compiler_params=pltpu.CompilerParams(vmem_limit_bytes=VMEM_LIMIT),
        cost_estimate=cost(4 * rows * units * (width + span * cols), 5e6, 2 * rows * units),
        name="projector",
    )(meta, own, other, first, *seconds)


def pick_kernel(spot, *refs):
    sources, out = refs[:-1], refs[-1]
    rows = out.shape[0]
    wanted = lax.broadcasted_iota(jnp.int32, (rows, spot.shape[1]), 0)
    at, total = 0, 0.0
    for ref in sources:
        count = ref.shape[0]
        picks = (spot[:, at : at + count] == wanted[:, at : at + count]).astype(F32).astype(BF16)
        total = total + dot(picks, ref[...])
        at += count
    out[...] = total.astype(BF16)


def pick_rows(spot, sources, rows):
    width = sources[0].shape[1]
    return pl.pallas_call(
        pick_kernel,
        out_shape=jax.ShapeDtypeStruct((rows, width), BF16),
        in_specs=[VMEM] * (1 + len(sources)),
        out_specs=VMEM,
        compiler_params=PARAMS,
        cost_estimate=cost(2 * rows * width * spot.shape[1], 2 * width * spot.shape[1]),
        name="pick_rows",
    )(spot, *sources)


def order_kernel(offsets, meta, keep, got, out):
    core, ctx = meta[1], meta[2]
    rows, count = out.shape[2], len(offsets)
    for i in range(2):
        for b, offset in enumerate(offsets):
            at = pl.ds((i * count + b) * rows, rows)
            there = pl.ds(((1 - i) * count + b) * rows, rows)
            total = keep[at, :].astype(F32) + got[there, :].astype(F32)
            out[ctx ^ offset, core ^ i] = total.astype(BF16)


def order_rows(meta, keep, got, offsets):
    rows, cols = keep.shape
    count = len(offsets)
    out = jax.ShapeDtypeStruct((count, 2, rows // count // 2, cols), BF16)
    return pl.pallas_call(
        functools.partial(order_kernel, tuple(offsets)),
        out_shape=out,
        in_specs=[SMEM, VMEM, VMEM],
        out_specs=VMEM,
        compiler_params=PARAMS,
        cost_estimate=cost(rows * cols, 6 * rows * cols),
        name="order_rows",
    )(meta, keep, got)


def image_norm_kernel(groups, span, heads, got, gain, out, total):
    wide = span // 2
    cols = got.shape[2] // wide
    square = 0.0
    for g in range(groups):
        for core in range(2):
            part = 0.0
            for s in range(span):
                for h in range(heads // 2):
                    part = part + got[((g * span + s) * heads) + 2 * h + core].astype(F32)
            part = part.astype(BF16).astype(F32)
            square = square + jnp.sum(part * part, axis=-1, keepdims=True)
            for n in range(wide):
                c = g * span + 2 * n + core
                total[:, c * cols : (c + 1) * cols] = part[:, n * cols : (n + 1) * cols]
    scale = lax.rsqrt(square / total.shape[1] + 1e-05)
    out[...] = (total[...] * scale * gain[...]).astype(BF16)


def image_norm(got, gain, n_ctx, span):
    devices, rows, _ = got.shape
    width = gain.shape[1]
    return pl.pallas_call(
        functools.partial(image_norm_kernel, n_ctx // span, span, devices // n_ctx),
        out_shape=jax.ShapeDtypeStruct((rows, width), BF16),
        in_specs=[VMEM, VMEM],
        out_specs=VMEM,
        scratch_shapes=[pltpu.VMEM((rows, width), F32)],
        compiler_params=PARAMS,
        cost_estimate=cost(4 * got.size, 2 * got.size),
        name="image_norm",
    )(got, gain)


def image_kernel(x, wq, wk, wv, text_state, out, state):
    rows = x[...]
    key = silu(dot(rows, wk[...])).astype(BF16)
    value = silu(dot(rows, wv[...])).astype(BF16)
    out[1] = key
    out[2] = value
    for h in range(state.shape[0]):
        cols = slice(h * HEAD_DIM, (h + 1) * HEAD_DIM)
        outer = lax.dot_general(
            key[:, cols], value[:, cols], (((0,), (0,)), ((), ())), preferred_element_type=F32
        )
        state[h] = (text_state[h] + outer).astype(BF16)
    out[0] = silu(dot(rows, wq[...])).astype(BF16)


def image_qkv(x, weights, text_state):
    rows, width = x.shape
    cols = weights[0].shape[1]
    return pl.pallas_call(
        image_kernel,
        out_shape=(
            jax.ShapeDtypeStruct((3, rows, cols), BF16),
            jax.ShapeDtypeStruct(text_state.shape, BF16),
        ),
        in_specs=[VMEM] * 5,
        out_specs=(VMEM, VMEM),
        compiler_params=PARAMS,
        cost_estimate=cost(6 * rows * width * cols, 6 * width * cols, 3 * rows * cols),
        name="image_qkv",
    )(x, *weights, text_state)


def finish_kernel(intra, q, state, gain, out):
    for h in range(state.shape[0]):
        cols = slice(h * HEAD_DIM, (h + 1) * HEAD_DIM)
        total = intra[:, cols] + dot(q[:, cols], state[h])
        scale = lax.rsqrt(jnp.mean(total * total, axis=-1, keepdims=True) + 1e-06)
        out[:, cols] = (total * scale * gain[:, cols]).astype(BF16)


def finish(intra, q, state, gain):
    rows, cols = q.shape
    return pl.pallas_call(
        finish_kernel,
        out_shape=jax.ShapeDtypeStruct((rows, cols), BF16),
        in_specs=[VMEM] * 4,
        out_specs=VMEM,
        compiler_params=PARAMS,
        cost_estimate=cost(2 * rows * cols * HEAD_DIM, 8 * rows * cols),
        name="finish",
    )(intra, q, state, gain)


def intra_kernel(text, image, put, q, out):
    where = put[...]
    for h in range(q.shape[1] // HEAD_DIM):
        at = slice(h * HEAD_DIM, (h + 1) * HEAD_DIM)
        queries, keys, values = [
            (text[n, :, at].astype(F32) + dot(where, image[n, :, at])).astype(BF16)
            for n in range(3)
        ]
        q[:, at] = queries
        scores = lax.dot_general(
            queries, keys, (((1,), (1,)), ((), ())), preferred_element_type=F32
        )
        rows = lax.broadcasted_iota(jnp.int32, scores.shape, 0)
        cols = lax.broadcasted_iota(jnp.int32, scores.shape, 1)
        scores = jnp.where(cols <= rows, scores, 0.0).astype(BF16)
        out[:, at] = dot(scores, values)


def intra_shard(text, image, put):
    _, rows, cols = text.shape
    return pl.pallas_call(
        intra_kernel,
        out_shape=(
            jax.ShapeDtypeStruct((rows, cols), BF16),
            jax.ShapeDtypeStruct((rows, cols), F32),
        ),
        in_specs=[VMEM] * 3,
        out_specs=(VMEM, VMEM),
        compiler_params=PARAMS,
        cost_estimate=cost(2e10, 4e7),
        name="intra_shard",
    )(text, image, put)


def turned(h, count):
    return (h >> 1) | ((h & 1) * (count // 2))


def mix_load_kernel(mix_offsets, meta, *refs):
    blocks, held, sems = refs[: len(mix_offsets)], refs[-2], refs[-1]
    ctx, head, ratio, count = meta[2], meta[3], meta[5], meta[6]
    base = ((head ^ turned(head, count)) * ratio) ^ ctx
    copies = []
    for n, offset in enumerate(mix_offsets):
        slot = base ^ offset
        copies.append(pltpu.make_async_copy(blocks[n], held.at[slot], sems.at[n]))
    for copy in copies:
        copy.start()
    for copy in copies:
        copy.wait()


def mix_load(meta, mix, mix_offsets):
    return pl.pallas_call(
        functools.partial(mix_load_kernel, tuple(mix_offsets)),
        out_shape=jax.ShapeDtypeStruct((len(mix),) + mix[0].shape, BF16),
        in_specs=[SMEM] + [ANYWHERE] * len(mix),
        out_specs=VMEM,
        scratch_shapes=[pltpu.SemaphoreType.DMA((len(mix),))],
        compiler_params=PARAMS,
        cost_estimate=cost(0, 4 * len(mix) * mix[0].size),
        name="mix_load",
    )(meta, *mix)


def mix_kernel(offsets, ratio, count, has_before, *refs):
    ins, (mix, *before, out) = refs[: len(offsets)], refs[len(offsets) :]
    cols = mix.shape[2]
    for r in range(ratio):
        to = slice(r * cols, (r + 1) * cols)
        total = before[0][:, to] if has_before else 0.0
        for ref, offset in zip(ins, offsets):
            total = total + dot(ref[...], mix[turned(offset, count) * ratio + r])
        out[:, to] = total.astype(out.dtype)


def mix_part(arrays, offsets, mix, ratio, count, before, dtype):
    rows, width = arrays[0].shape
    cols = mix.shape[2]
    extra = [] if before is None else [before]
    return pl.pallas_call(
        functools.partial(mix_kernel, tuple(offsets), ratio, count, before is not None),
        out_shape=jax.ShapeDtypeStruct((rows, ratio * cols), dtype),
        in_specs=[VMEM] * (len(arrays) + 1 + len(extra)),
        out_specs=VMEM,
        compiler_params=PARAMS,
        cost_estimate=cost(2 * rows * width * ratio * cols * len(arrays), 5e6),
        name="mix_part",
    )(*arrays, mix, *extra)


def on_device(
    enc_rows,
    row_counts,
    row_places,
    stream,
    norm_gain,
    proj_in,
    proj_out,
    qkv_weight,
    head_gain,
    mix_weight,
):
    both = ("ctx", "head")
    capacity, enc_width = enc_rows.shape
    shard_rows, width = stream.shape
    n_ctx, n_head = lax.axis_size("ctx"), lax.axis_size("head")
    ctx, head = lax.axis_index("ctx"), lax.axis_index("head")
    live_total = n_head * (capacity // 4)
    core_rows = live_total // 2
    part_rows = live_total // n_head
    n_pairs = n_ctx // 2
    core, parity = head & 1, ctx & 1
    span = 4
    spot_in = ctx & (span - 1)
    ratio = n_ctx // n_head
    meta = jnp.stack([parity, core, ctx, head, spot_in, ratio, n_head]).astype(jnp.int32)
    flat = [(c, h) for c in range(n_ctx) for h in range(n_head)]

    def along(axis, count, mask):
        return functools.partial(
            lax.ppermute, axis_name=axis, perm=[(i, i ^ mask) for i in range(count)]
        )

    def index(c, h):
        return c * n_head + h

    perm = [(index(c, h), index(c ^ (turned(h, n_head) * ratio), h)) for c, h in flat]
    mix_own = lax.ppermute(mix_weight, both, perm)

    part = proj_in.shape[1] // span
    if part % 128 == 0:
        in_sends = spread_units(proj_in, n_ctx, span)
    else:
        in_sends = jnp.stack([proj_in[:, c % span * part :][:, :part] for c in range(n_ctx)])
    out_cols = proj_out.shape[1]

    sources, swaps = [enc_rows], [0]
    bit = n_head // 2
    while bit:
        sources = sources + [along("head", n_head, bit)(x) for x in sources]
        swaps = swaps + [o ^ bit for o in swaps]
        bit //= 2
    counts = row_counts[0]
    earlier = jnp.arange(n_head)[:, None] > jnp.arange(n_head)[None, :]
    starts = jnp.sum(jnp.where(earlier, counts[None, :], 0), axis=1)
    within = jnp.arange(capacity, dtype=jnp.int32)[None, :]
    spot = jnp.where(within < counts[:, None], starts[:, None] + within, -1)
    owners = jnp.arange(n_head)[None, :] == (head ^ jnp.array(swaps, dtype=jnp.int32))[:, None]
    swapped = jnp.sum(jnp.where(owners[:, :, None], spot[None], 0), axis=1)
    own_rows = pick_rows(swapped.reshape(1, -1) - core * core_rows, sources, core_rows)
    own_rows, in_sends = lax.optimization_barrier((own_rows, in_sends))
    (in_full,) = weighty([lax.all_to_all(in_sends, "ctx", 0, 0)], 1e11, 4e8)
    in_full = in_full.reshape(enc_width, part)

    def norm(rows):
        widened = rows.astype(F32)
        return (
            widened
            * lax.rsqrt(jnp.mean(widened * widened, axis=-1, keepdims=True) + 1e-05)
            * norm_gain
        ).astype(BF16)

    def spread(x, mask):
        return jnp.concatenate([x, along("ctx", n_ctx, mask)(x)])

    masks = [1 << n for n in reversed(range(n_ctx.bit_length() - 1))]
    masks = masks[-1:] + masks[:-1]
    offsets_ctx = [0]
    for mask in masks:
        offsets_ctx = offsets_ctx + [o ^ mask for o in offsets_ctx]
    core_part, proj_out, stream, mix_own = lax.optimization_barrier(
        (spread(own_rows, masks[0]), proj_out, stream, mix_own)
    )
    perm = [(index(c, h), index(c, (c // ratio) ^ turned(h, n_head))) for c, h in flat]
    mix_own = lax.ppermute(mix_own, both, perm)
    text_rows = norm(stream)

    seconds = []
    for m in range(span):
        block = lax.dynamic_slice(proj_out, ((spot_in ^ m) * part, 0), (part, out_cols))
        seconds.append(along("ctx", n_ctx, m)(block) if m else block)
    seconds = weighty(seconds, 4e10, 1.6e8)

    core_part = spread(core_part, masks[1])
    core_part, mix_own, text_rows, qkv_weight = lax.optimization_barrier(
        (core_part, mix_own, text_rows, qkv_weight)
    )
    weights = [qkv_weight[:, i, :] for i in range(3)]
    for mask in masks[2:]:
        core_part = spread(core_part, mask)
    core_part, mix_own, weights = lax.optimization_barrier((core_part, mix_own, weights))
    other_part = along("head", n_head, 1)(core_part)

    mix_blocks = {0: mix_own}
    top = n_ctx // 2
    single = [o for o in range(1, top) if o & (o - 1) == 0]
    double = [o for o in range(1, top) if o not in single]
    late = [o for o in range(top + 1, n_ctx) if o & 1 == 0 or o == top + 1]
    last = [o for o in range(top + 1, n_ctx) if o not in late]

    def mix_start(stage):
        for offset in stage:
            mask = offset & -offset
            mix_blocks[offset] = along("ctx", n_ctx, mask)(mix_blocks[offset ^ mask])

    def mix_end(stage, beside):
        arrays, beside = lax.optimization_barrier(([mix_blocks[o] for o in stage], beside))
        mix_blocks.update(zip(stage, arrays))
        return beside

    mix_start(single)

    keep, send = projector(meta, core_part, other_part, in_full, seconds)
    ordered = order_rows(meta, keep, along("head", n_head, 1)(send), offsets_ctx)
    ordered, text_rows, weights = lax.optimization_barrier((ordered, text_rows, weights))
    local_places = row_places[0] - ctx * shard_rows
    picks = spot.reshape(1, -1) == jnp.arange(live_total, dtype=jnp.int32)[:, None]
    places = jnp.sum(jnp.where(picks, local_places[None, :], 0), axis=1)
    put = jnp.arange(shard_rows, dtype=jnp.int32)[:, None] == places[None, :]
    is_text = jnp.logical_not(jnp.any(put, axis=1))[:, None]

    text, text_state = mix_end(
        single, text_qkv(text_rows, is_text.astype(F32), weights)
    )
    mix_start(double)

    received = lax.all_to_all(
        ordered.reshape(n_ctx * n_head, part_rows, span // 2 * out_cols), both, 0, 0
    )
    (received,) = weighty([received], 2e11, 8e8)
    received, text = mix_end([0], (received, text))
    mix_start([top])

    if out_cols % 128 == 0:
        img_part = image_norm(received, norm_gain[None], n_ctx, span)
    else:
        received = received.reshape(
            n_ctx // span, span, n_head // 2, 2, part_rows, span // 2, out_cols
        )
        summed = jnp.sum(received.astype(F32), axis=(1, 2)).astype(BF16)
        img_part = norm(summed.transpose(2, 0, 3, 1, 4).reshape(part_rows, width))
    image_rows = lax.all_gather(img_part, "head", axis=0, tiled=True)

    image, state = image_qkv(image_rows, weights, text_state)
    state = mix_end([top] + double, state)
    mix_start(late)

    pieces = lax.all_to_all(state.reshape(n_ctx, -1, HEAD_DIM), "ctx", 0, 0).astype(F32)
    before = (jnp.cumsum(pieces, axis=0) - pieces).astype(BF16)
    before, put = lax.optimization_barrier((before, put.astype(BF16)))
    prefix = lax.all_to_all(before, "ctx", 0, 0).reshape(state.shape)

    queries, intra = mix_end(late, intra_shard(text, image, put))
    mix_start(last)
    heads_out = finish(intra, queries, prefix, head_gain[None])

    mix_cols = mix_weight.shape[1]
    near, near_offsets = [heads_out], [0]
    near.append(along("head", n_head, 1)(heads_out))
    near_offsets.append(1)
    far, far_offsets = [], []
    bit = n_head // 2
    sent, sent_offsets = [heads_out], [0]
    while bit > 1:
        sent = sent + [along("head", n_head, bit)(p) for p in sent]
        sent_offsets = sent_offsets + [o ^ bit for o in sent_offsets]
        bit //= 2
    near = mix_end(last, near)
    mix_offsets, mix_blocks = list(mix_blocks), list(mix_blocks.values())
    first = None
    if mix_cols % 128 == 0:
        mix_full = mix_load(meta, mix_blocks, mix_offsets)
        first = mix_part(near, near_offsets, mix_full, ratio, n_head, None, F32)
        sent, first = lax.optimization_barrier((sent, first))
    far = sent[1:] + [along("head", n_head, 1)(p) for p in sent[1:]]
    far_offsets = sent_offsets[1:] + [o ^ 1 for o in sent_offsets[1:]]
    if mix_cols % 128 == 0:
        return mix_part(far, far_offsets, mix_full, ratio, n_head, first, BF16)
    parts, offsets = near + far, near_offsets + far_offsets
    mix_full = jnp.stack([mix_blocks[mix_offsets.index(o)] for o in range(n_ctx)])
    total = 0.0
    for part, offset in zip(parts, offsets):
        spot = head ^ turned(head ^ offset, n_head)
        group = [
            lax.dynamic_index_in_dim(mix_full, (spot * ratio + r) ^ ctx, 0, keepdims=False)
            for r in range(ratio)
        ]
        total = total + dot(part, jnp.concatenate(group, axis=1))
    return total.astype(BF16)


def solution(mesh):
    in_specs = (
        P(("ctx", "head"), None),
        P("ctx", None),
        P("ctx", None),
        P("ctx", None),
        P(),
        P("ctx", "head"),
        P("head", "ctx"),
        P(None, None, "head"),
        P("head"),
        P("head", "ctx"),
    )
    out_specs = P("ctx", "head")
    return jax.shard_map(
        on_device, mesh=mesh, in_specs=in_specs, out_specs=out_specs, check_vma=False
    )
```

```python
import functools

import jax
import jax.numpy as jnp
from jax import lax
from jax.experimental import pallas as pl
from jax.experimental.pallas import tpu as pltpu
from jax.sharding import PartitionSpec as P

HEAD_DIM = 128
F32 = jnp.float32
BF16 = jnp.bfloat16
VMEM_LIMIT = 20 * 1024 * 1024
VMEM = pl.BlockSpec(memory_space=pltpu.VMEM)
SMEM = pl.BlockSpec(memory_space=pltpu.SMEM)
ANYWHERE = pl.BlockSpec(memory_space=pl.ANY)
HBM = pl.BlockSpec(memory_space=pltpu.HBM)
PARAMS = pltpu.CompilerParams(vmem_limit_bytes=VMEM_LIMIT)
FETCHING = pltpu.CompilerParams(vmem_limit_bytes=56 * 1024 * 1024)


def cost(flops, nbytes, transcendentals=0):
    return pl.CostEstimate(
        flops=int(flops), bytes_accessed=int(nbytes), transcendentals=int(transcendentals)
    )


def dot(a, b):
    return jnp.dot(a, b, preferred_element_type=F32)


def silu(x):
    return x * (1.0 / (1.0 + jnp.exp(-x)))


def nothing(*refs):
    pass


def weighty(arrays, flops, nbytes):
    anywhere = pl.BlockSpec(memory_space=pl.ANY)
    return pl.pallas_call(
        nothing,
        out_shape=[jax.ShapeDtypeStruct(x.shape, x.dtype) for x in arrays],
        in_specs=[anywhere] * len(arrays),
        out_specs=[anywhere] * len(arrays),
        input_output_aliases={i: i for i in range(len(arrays))},
        cost_estimate=cost(flops, nbytes),
        name="weighty",
    )(*arrays)


def spread_kernel(span, x, out):
    part = out.shape[2]
    for c in range(out.shape[0]):
        at = c % span * part
        out[c] = x[:, at : at + part]


def spread_units(x, n_ctx, span):
    rows, units = x.shape
    return pl.pallas_call(
        functools.partial(spread_kernel, span),
        out_shape=jax.ShapeDtypeStruct((n_ctx, rows, units // span), x.dtype),
        in_specs=[VMEM],
        out_specs=VMEM,
        compiler_params=PARAMS,
        cost_estimate=cost(0, 4 * x.size),
        name="spread_units",
    )(x)


def text_kernel(rows, keep, wq, wk, wv, out, state):
    step = min(rows.shape[0], 256)
    for i in range(rows.shape[0] // step):
        at = slice(i * step, (i + 1) * step)
        for n, w in enumerate((wq, wk, wv)):
            out[n, at, :] = (silu(dot(rows[at, :], w[...])) * keep[at, :]).astype(BF16)
    for h in range(state.shape[0]):
        cols = slice(h * HEAD_DIM, (h + 1) * HEAD_DIM)
        state[h] = lax.dot_general(
            out[1, :, cols], out[2, :, cols], (((0,), (0,)), ((), ())), preferred_element_type=F32
        )


def text_qkv(rows, keep, weights):
    count, width = rows.shape
    cols = weights[0].shape[1]
    heads = cols // HEAD_DIM
    return pl.pallas_call(
        text_kernel,
        out_shape=(
            jax.ShapeDtypeStruct((3, count, cols), BF16),
            jax.ShapeDtypeStruct((heads, HEAD_DIM, HEAD_DIM), F32),
        ),
        in_specs=[VMEM] * 5,
        out_specs=(VMEM, VMEM),
        compiler_params=PARAMS,
        cost_estimate=cost(6 * count * width * cols, 6 * width * cols, 3 * count * cols),
        name="text_qkv",
    )(rows, keep, *weights)


def projector_kernel(chunk, span, pieces, meta, *refs):
    sources, refs = refs[:pieces], refs[pieces:]
    first_hbm, refs = refs[0], refs[1:]
    seconds_hbm, refs = refs[:span], refs[span:]
    keep, send, held, first, seconds, w_keep, w_send, sems = refs
    count = sources[0].shape[0]
    copies = [pltpu.make_async_copy(first_hbm, first, sems.at[0])]
    for n, source in enumerate(sources):
        to = held.at[n * count : (n + 1) * count, :]
        copies.append(pltpu.make_async_copy(source, to, sems.at[1 + n]))
    for m in range(span):
        copies.append(
            pltpu.make_async_copy(seconds_hbm[m], seconds.at[m], sems.at[1 + pieces + m])
        )
    for copy in copies:
        copy.start()
    for copy in copies:
        copy.wait()
    cols = seconds.shape[2]
    same = meta[0] == meta[1]
    for m in range(0, span, 2):
        mine, near = seconds[m], seconds[m + 1]
        slot = (meta[4] ^ m) >> 1
        w_keep[slot] = jnp.where(same, mine, near)
        w_send[slot] = jnp.where(same, near, mine)

    @pl.loop(0, held.shape[0] // chunk)
    def _(i):
        at = pl.ds(pl.multiple_of(i * chunk, chunk), chunk)
        pre = dot(held[at, :], first[...])
        hid = (0.5 * pre * (1.0 + lax.erf(pre * 0.7071067811865476))).astype(BF16)
        for n in range(span // 2):
            keep[at, n * cols : (n + 1) * cols] = dot(hid, w_keep[n]).astype(BF16)
            send[at, n * cols : (n + 1) * cols] = dot(hid, w_send[n]).astype(BF16)


def projector(meta, sources, first, seconds):
    rows, width = sources[0].shape
    rows = rows * len(sources)
    units, cols = seconds[0].shape
    span = len(seconds)
    out = jax.ShapeDtypeStruct((rows, span // 2 * cols), BF16)
    side = pltpu.VMEM((span // 2, units, cols), BF16)
    return pl.pallas_call(
        functools.partial(projector_kernel, min(rows, 256), span, len(sources)),
        out_shape=(out, out),
        in_specs=[SMEM] + [HBM] * (len(sources) + 1 + span),
        out_specs=(VMEM, VMEM),
        scratch_shapes=[
            pltpu.VMEM((rows, width), BF16),
            pltpu.VMEM((width, units), BF16),
            pltpu.VMEM((span, units, cols), BF16),
            side,
            side,
            pltpu.SemaphoreType.DMA((1 + len(sources) + span,)),
        ],
        compiler_params=FETCHING,
        cost_estimate=cost(2 * rows * units * (width + span * cols), 5e6, rows * units),
        name="projector",
    )(meta, *sources, first, *seconds)


def pick_kernel(spot, *refs):
    sources, out = refs[:-1], refs[-1]
    rows = out.shape[0]
    wanted = lax.broadcasted_iota(jnp.int32, (rows, spot.shape[1]), 0)
    at, total = 0, 0.0
    for ref in sources:
        count = ref.shape[0]
        picks = (spot[:, at : at + count] == wanted[:, at : at + count]).astype(F32).astype(BF16)
        total = total + dot(picks, ref[...])
        at += count
    out[...] = total.astype(BF16)


def pick_rows(spot, sources, rows):
    width = sources[0].shape[1]
    return pl.pallas_call(
        pick_kernel,
        out_shape=jax.ShapeDtypeStruct((rows, width), BF16),
        in_specs=[VMEM] * (1 + len(sources)),
        out_specs=VMEM,
        compiler_params=PARAMS,
        cost_estimate=cost(2 * rows * width * spot.shape[1], 2 * width * spot.shape[1]),
        name="pick_rows",
    )(spot, *sources)


def order_kernel(offsets, meta, keep, got, out):
    core, ctx = meta[1], meta[2]
    rows, count = out.shape[2], len(offsets)
    for i in range(2):
        for b, offset in enumerate(offsets):
            at = pl.ds((i * count + b) * rows, rows)
            there = pl.ds(((1 - i) * count + b) * rows, rows)
            total = keep[at, :].astype(F32) + got[there, :].astype(F32)
            out[ctx ^ offset, core ^ i] = total.astype(BF16)


def order_rows(meta, keep, got, offsets):
    rows, cols = keep.shape
    count = len(offsets)
    out = jax.ShapeDtypeStruct((count, 2, rows // count // 2, cols), BF16)
    return pl.pallas_call(
        functools.partial(order_kernel, tuple(offsets)),
        out_shape=out,
        in_specs=[SMEM, VMEM, VMEM],
        out_specs=VMEM,
        compiler_params=PARAMS,
        cost_estimate=cost(rows * cols, 6 * rows * cols),
        name="order_rows",
    )(meta, keep, got)


def image_norm_kernel(groups, span, heads, got, gain, out, total):
    wide = span // 2
    cols = got.shape[2] // wide
    square = 0.0
    for g in range(groups):
        for core in range(2):
            part = 0.0
            for s in range(span):
                for h in range(heads // 2):
                    part = part + got[((g * span + s) * heads) + 2 * h + core].astype(F32)
            part = part.astype(BF16).astype(F32)
            square = square + jnp.sum(part * part, axis=-1, keepdims=True)
            for n in range(wide):
                c = g * span + 2 * n + core
                total[:, c * cols : (c + 1) * cols] = part[:, n * cols : (n + 1) * cols]
    scale = lax.rsqrt(square / total.shape[1] + 1e-05)
    out[...] = (total[...] * scale * gain[...]).astype(BF16)


def image_norm(got, gain, n_ctx, span):
    devices, rows, _ = got.shape
    width = gain.shape[1]
    return pl.pallas_call(
        functools.partial(image_norm_kernel, n_ctx // span, span, devices // n_ctx),
        out_shape=jax.ShapeDtypeStruct((rows, width), BF16),
        in_specs=[VMEM, VMEM],
        out_specs=VMEM,
        scratch_shapes=[pltpu.VMEM((rows, width), F32)],
        compiler_params=PARAMS,
        cost_estimate=cost(4 * got.size, 2 * got.size),
        name="image_norm",
    )(got, gain)


def image_kernel(steps, x, wq, wk, wv, text_state, out, state, held, sems):
    rows = x[...]
    depth = x.shape[1] // steps
    order = ((1, wk), (2, wv), (0, wq))

    def copy(n, w, i):
        at = slice(i * depth, (i + 1) * depth)
        return pltpu.make_async_copy(w.at[at, :], held.at[n, at, :], sems.at[n * steps + i])

    for n, w in order:
        for i in range(steps):
            copy(n, w, i).start()
    for n, w in order:
        total = 0.0
        for i in range(steps):
            copy(n, w, i).wait()
            at = slice(i * depth, (i + 1) * depth)
            total = total + dot(rows[:, at], held[n, at, :])
        out[n] = silu(total).astype(BF16)
    for h in range(state.shape[0]):
        cols = slice(h * HEAD_DIM, (h + 1) * HEAD_DIM)
        outer = lax.dot_general(
            out[1, :, cols], out[2, :, cols], (((0,), (0,)), ((), ())), preferred_element_type=F32
        )
        state[h] = (text_state[h] + outer).astype(BF16)


def image_qkv(x, weights, text_state):
    rows, width = x.shape
    cols = weights[0].shape[1]
    steps = 4 if width % 1024 == 0 else 1
    return pl.pallas_call(
        functools.partial(image_kernel, steps),
        out_shape=(
            jax.ShapeDtypeStruct((3, rows, cols), BF16),
            jax.ShapeDtypeStruct(text_state.shape, BF16),
        ),
        in_specs=[VMEM] + [HBM] * 3 + [VMEM],
        out_specs=(VMEM, VMEM),
        scratch_shapes=[
            pltpu.VMEM((3, width, cols), BF16),
            pltpu.SemaphoreType.DMA((3 * steps,)),
        ],
        compiler_params=FETCHING,
        cost_estimate=cost(6 * rows * width * cols, 6 * width * cols, 3 * rows * cols),
        name="image_qkv",
    )(x, *weights, text_state)


def finish_kernel(intra, q, state, gain, out):
    for h in range(state.shape[0]):
        cols = slice(h * HEAD_DIM, (h + 1) * HEAD_DIM)
        total = intra[:, cols] + dot(q[:, cols], state[h])
        scale = lax.rsqrt(jnp.mean(total * total, axis=-1, keepdims=True) + 1e-06)
        out[:, cols] = (total * scale * gain[:, cols]).astype(BF16)


def finish(intra, q, state, gain):
    rows, cols = q.shape
    return pl.pallas_call(
        finish_kernel,
        out_shape=jax.ShapeDtypeStruct((rows, cols), BF16),
        in_specs=[VMEM] * 4,
        out_specs=VMEM,
        compiler_params=PARAMS,
        cost_estimate=cost(2 * rows * cols * HEAD_DIM, 8 * rows * cols),
        name="finish",
    )(intra, q, state, gain)


def intra_kernel(text, image, put, q, out):
    where = put[...]
    for h in range(q.shape[1] // HEAD_DIM):
        at = slice(h * HEAD_DIM, (h + 1) * HEAD_DIM)
        queries, keys, values = [
            (text[n, :, at].astype(F32) + dot(where, image[n, :, at])).astype(BF16)
            for n in range(3)
        ]
        q[:, at] = queries
        scores = lax.dot_general(
            queries, keys, (((1,), (1,)), ((), ())), preferred_element_type=F32
        )
        rows = lax.broadcasted_iota(jnp.int32, scores.shape, 0)
        cols = lax.broadcasted_iota(jnp.int32, scores.shape, 1)
        scores = jnp.where(cols <= rows, scores, 0.0).astype(BF16)
        out[:, at] = dot(scores, values)


def intra_shard(text, image, put):
    _, rows, cols = text.shape
    return pl.pallas_call(
        intra_kernel,
        out_shape=(
            jax.ShapeDtypeStruct((rows, cols), BF16),
            jax.ShapeDtypeStruct((rows, cols), F32),
        ),
        in_specs=[VMEM] * 3,
        out_specs=(VMEM, VMEM),
        compiler_params=PARAMS,
        cost_estimate=cost(2e10, 4e7),
        name="intra_shard",
    )(text, image, put)


def turned(h, count):
    return (h >> 1) | ((h & 1) * (count // 2))


def mix_load_kernel(mix_offsets, meta, *refs):
    blocks, held, sems = refs[: len(mix_offsets)], refs[-2], refs[-1]
    ctx, head, ratio, count = meta[2], meta[3], meta[5], meta[6]
    base = ((head ^ turned(head, count)) * ratio) ^ ctx
    copies = []
    for n, offset in enumerate(mix_offsets):
        slot = base ^ offset
        copies.append(pltpu.make_async_copy(blocks[n], held.at[slot], sems.at[n]))
    for copy in copies:
        copy.start()
    for copy in copies:
        copy.wait()


def mix_load(meta, mix, mix_offsets):
    return pl.pallas_call(
        functools.partial(mix_load_kernel, tuple(mix_offsets)),
        out_shape=jax.ShapeDtypeStruct((len(mix),) + mix[0].shape, BF16),
        in_specs=[SMEM] + [HBM] * len(mix),
        out_specs=VMEM,
        scratch_shapes=[pltpu.SemaphoreType.DMA((len(mix),))],
        compiler_params=PARAMS,
        cost_estimate=cost(0, 4 * len(mix) * mix[0].size),
        name="mix_load",
    )(meta, *mix)


def mix_kernel(offsets, ratio, count, has_before, *refs):
    ins, (mix, *before, out) = refs[: len(offsets)], refs[len(offsets) :]
    cols = mix.shape[2]
    for r in range(ratio):
        to = slice(r * cols, (r + 1) * cols)
        total = before[0][:, to] if has_before else 0.0
        for ref, offset in zip(ins, offsets):
            total = total + dot(ref[...], mix[turned(offset, count) * ratio + r])
        out[:, to] = total.astype(out.dtype)


def mix_part(arrays, offsets, mix, ratio, count, before, dtype):
    rows, width = arrays[0].shape
    cols = mix.shape[2]
    extra = [] if before is None else [before]
    return pl.pallas_call(
        functools.partial(mix_kernel, tuple(offsets), ratio, count, before is not None),
        out_shape=jax.ShapeDtypeStruct((rows, ratio * cols), dtype),
        in_specs=[VMEM] * (len(arrays) + 1 + len(extra)),
        out_specs=VMEM,
        compiler_params=PARAMS,
        cost_estimate=cost(2 * rows * width * ratio * cols * len(arrays), 5e6),
        name="mix_part",
    )(*arrays, mix, *extra)


def on_device(
    enc_rows,
    row_counts,
    row_places,
    stream,
    norm_gain,
    proj_in,
    proj_out,
    qkv_weight,
    head_gain,
    mix_weight,
):
    both = ("ctx", "head")
    capacity, enc_width = enc_rows.shape
    shard_rows, width = stream.shape
    n_ctx, n_head = lax.axis_size("ctx"), lax.axis_size("head")
    ctx, head = lax.axis_index("ctx"), lax.axis_index("head")
    live_total = n_head * (capacity // 4)
    core_rows = live_total // 2
    part_rows = live_total // n_head
    n_pairs = n_ctx // 2
    core, parity = head & 1, ctx & 1
    span = 2
    spot_in = ctx & (span - 1)
    ratio = n_ctx // n_head
    meta = jnp.stack([parity, core, ctx, head, spot_in, ratio, n_head]).astype(jnp.int32)
    flat = [(c, h) for c in range(n_ctx) for h in range(n_head)]

    def along(axis, count, mask):
        return functools.partial(
            lax.ppermute, axis_name=axis, perm=[(i, i ^ mask) for i in range(count)]
        )

    def index(c, h):
        return c * n_head + h

    perm = [(index(c, h), index(c ^ (turned(h, n_head) * ratio), h)) for c, h in flat]
    mix_own = lax.ppermute(mix_weight, both, perm)

    part = proj_in.shape[1] // span
    if part % 128 == 0:
        in_sends = spread_units(proj_in, n_ctx, span)
    else:
        in_sends = jnp.stack([proj_in[:, c % span * part :][:, :part] for c in range(n_ctx)])
    out_cols = proj_out.shape[1]

    sources, swaps = [enc_rows], [0]
    bit = n_head // 2
    while bit:
        sources = sources + [along("head", n_head, bit)(x) for x in sources]
        swaps = swaps + [o ^ bit for o in swaps]
        bit //= 2
    counts = row_counts[0]
    earlier = jnp.arange(n_head)[:, None] > jnp.arange(n_head)[None, :]
    starts = jnp.sum(jnp.where(earlier, counts[None, :], 0), axis=1)
    within = jnp.arange(capacity, dtype=jnp.int32)[None, :]
    spot = jnp.where(within < counts[:, None], starts[:, None] + within, -1)
    owners = jnp.arange(n_head)[None, :] == (head ^ jnp.array(swaps, dtype=jnp.int32))[:, None]
    swapped = jnp.sum(jnp.where(owners[:, :, None], spot[None], 0), axis=1)
    own_rows = pick_rows(swapped.reshape(1, -1) - core * core_rows, sources, core_rows)
    own_rows, in_sends = lax.optimization_barrier((own_rows, in_sends))
    (in_full,) = weighty([lax.all_to_all(in_sends, "ctx", 0, 0)], 1e11, 4e8)
    in_full = in_full.reshape(enc_width, part)

    def norm(rows):
        widened = rows.astype(F32)
        return (
            widened
            * lax.rsqrt(jnp.mean(widened * widened, axis=-1, keepdims=True) + 1e-05)
            * norm_gain
        ).astype(BF16)

    def spread(x, mask):
        return jnp.concatenate([x, along("ctx", n_ctx, mask)(x)])

    masks = [1 << n for n in reversed(range(n_ctx.bit_length() - 1))]
    offsets_ctx = [0]
    for mask in masks:
        offsets_ctx = offsets_ctx + [o ^ mask for o in offsets_ctx]
    core_part, proj_out, mix_own, stream, qkv_weight = lax.optimization_barrier(
        (spread(own_rows, masks[0]), proj_out, mix_own, stream, qkv_weight)
    )
    perm = [(index(c, h), index(c, (c // ratio) ^ turned(h, n_head))) for c, h in flat]
    mix_own = lax.ppermute(mix_own, both, perm)

    seconds = []
    for m in range(span):
        block = lax.dynamic_slice(proj_out, ((spot_in ^ m) * part, 0), (part, out_cols))
        seconds.append(block)
    seconds = [along("ctx", n_ctx, m)(x) if m else x for m, x in enumerate(seconds)]
    seconds = weighty(seconds, 1e10, 4e7)
    text_rows = norm(stream)
    weights = [qkv_weight[:, i, :] for i in range(3)]
    local_places = row_places[0] - ctx * shard_rows
    picks = spot.reshape(1, -1) == jnp.arange(live_total, dtype=jnp.int32)[:, None]
    places = jnp.sum(jnp.where(picks, local_places[None, :], 0), axis=1)
    put = jnp.arange(shard_rows, dtype=jnp.int32)[:, None] == places[None, :]
    is_text = jnp.logical_not(jnp.any(put, axis=1))[:, None]

    text, text_state = text_qkv(text_rows, is_text.astype(F32), weights)

    core_part = spread(core_part, masks[1])
    core_part, mix_own, text = lax.optimization_barrier((core_part, mix_own, text))
    for mask in masks[2:-1]:
        core_part = spread(core_part, mask)
    core_parts = [core_part, along("ctx", n_ctx, masks[-1])(core_part)]
    other_parts = [along("head", n_head, 1)(x) for x in core_parts]
    core_parts, mix_own = lax.optimization_barrier((core_parts, mix_own))

    mix_blocks = {0: mix_own}
    top = n_ctx // 2
    single = [o for o in range(1, top) if o & (o - 1) == 0]
    double = [o for o in range(1, top) if o not in single]
    late = [o for o in range(top + 1, n_ctx) if o & 1 == 0 or o == top + 1]
    last = [o for o in range(top + 1, n_ctx) if o not in late]

    def mix_start(stage):
        for offset in stage:
            mask = offset & -offset
            mix_blocks[offset] = along("ctx", n_ctx, mask)(mix_blocks[offset ^ mask])

    def mix_end(stage, beside):
        arrays, beside = lax.optimization_barrier(([mix_blocks[o] for o in stage], beside))
        mix_blocks.update(zip(stage, arrays))
        return beside

    mix_start(single)

    keep, send = projector(meta, core_parts + other_parts, in_full, seconds)
    ordered = order_rows(meta, keep, along("head", n_head, 1)(send), offsets_ctx)
    ordered, mix_blocks[0] = lax.optimization_barrier((ordered, mix_blocks[0]))
    mix_start([top])

    received = lax.all_to_all(
        ordered.reshape(n_ctx * n_head, part_rows, span // 2 * out_cols), both, 0, 0
    )
    (received,) = weighty([received], 2e11, 8e8)

    if out_cols % 128 == 0:
        img_part = image_norm(received, norm_gain[None], n_ctx, span)
    else:
        received = received.reshape(
            n_ctx // span, span, n_head // 2, 2, part_rows, span // 2, out_cols
        )
        summed = jnp.sum(received.astype(F32), axis=(1, 2)).astype(BF16)
        img_part = norm(summed.transpose(2, 0, 3, 1, 4).reshape(part_rows, width))
    image_rows = lax.all_gather(img_part, "head", axis=0, tiled=True)

    image_rows = mix_end(single, image_rows)
    mix_start(double)
    image, state = image_qkv(image_rows, weights, text_state)
    state = mix_end([top], state)
    mix_start(late)

    pieces = lax.all_to_all(state.reshape(n_ctx, -1, HEAD_DIM), "ctx", 0, 0).astype(F32)
    before = (jnp.cumsum(pieces, axis=0) - pieces).astype(BF16)
    before, put = lax.optimization_barrier((before, put.astype(BF16)))
    prefix = lax.all_to_all(before, "ctx", 0, 0).reshape(state.shape)

    queries, intra = mix_end(double + late, intra_shard(text, image, put))
    mix_start(last)
    heads_out = finish(intra, queries, prefix, head_gain[None])

    mix_cols = mix_weight.shape[1]
    near, near_offsets = [heads_out], [0]
    near.append(along("head", n_head, 1)(heads_out))
    near_offsets.append(1)
    far, far_offsets = [], []
    bit = n_head // 2
    sent, sent_offsets = [heads_out], [0]
    while bit > 1:
        sent = sent + [along("head", n_head, bit)(p) for p in sent]
        sent_offsets = sent_offsets + [o ^ bit for o in sent_offsets]
        bit //= 2
    near, sent = mix_end(last, (near, sent))
    mix_offsets, mix_blocks = list(mix_blocks), list(mix_blocks.values())
    first = None
    if mix_cols % 128 == 0:
        mix_full = mix_load(meta, mix_blocks, mix_offsets)
        first = mix_part(near, near_offsets, mix_full, ratio, n_head, None, F32)
    far = sent[1:] + [along("head", n_head, 1)(p) for p in sent[1:]]
    far_offsets = sent_offsets[1:] + [o ^ 1 for o in sent_offsets[1:]]
    if mix_cols % 128 == 0:
        return mix_part(far, far_offsets, mix_full, ratio, n_head, first, BF16)
    parts, offsets = near + far, near_offsets + far_offsets
    mix_full = jnp.stack([mix_blocks[mix_offsets.index(o)] for o in range(n_ctx)])
    total = 0.0
    for part, offset in zip(parts, offsets):
        spot = head ^ turned(head ^ offset, n_head)
        group = [
            lax.dynamic_index_in_dim(mix_full, (spot * ratio + r) ^ ctx, 0, keepdims=False)
            for r in range(ratio)
        ]
        total = total + dot(part, jnp.concatenate(group, axis=1))
    return total.astype(BF16)


def solution(mesh):
    in_specs = (
        P(("ctx", "head"), None),
        P("ctx", None),
        P("ctx", None),
        P("ctx", None),
        P(),
        P("ctx", "head"),
        P("head", "ctx"),
        P(None, None, "head"),
        P("head"),
        P("head", "ctx"),
    )
    out_specs = P("ctx", "head")
    return jax.shard_map(
        on_device, mesh=mesh, in_specs=in_specs, out_specs=out_specs, check_vma=False
    )
```

```python
import functools

import jax
import jax.numpy as jnp
from jax import lax
from jax.experimental import pallas as pl
from jax.experimental.pallas import tpu as pltpu
from jax.sharding import PartitionSpec as P

HEAD_DIM = 128
F32 = jnp.float32
BF16 = jnp.bfloat16
VMEM_LIMIT = 20 * 1024 * 1024
VMEM = pl.BlockSpec(memory_space=pltpu.VMEM)
SMEM = pl.BlockSpec(memory_space=pltpu.SMEM)
ANYWHERE = pl.BlockSpec(memory_space=pl.ANY)
HBM = pl.BlockSpec(memory_space=pltpu.HBM)
PARAMS = pltpu.CompilerParams(vmem_limit_bytes=VMEM_LIMIT)
FETCHING = pltpu.CompilerParams(vmem_limit_bytes=56 * 1024 * 1024)


def cost(flops, nbytes, transcendentals=0):
    return pl.CostEstimate(
        flops=int(flops), bytes_accessed=int(nbytes), transcendentals=int(transcendentals)
    )


def dot(a, b):
    return jnp.dot(a, b, preferred_element_type=F32)


def silu(x):
    return x * (1.0 / (1.0 + jnp.exp(-x)))


def nothing(*refs):
    pass


def weighty(arrays, flops, nbytes):
    anywhere = pl.BlockSpec(memory_space=pl.ANY)
    return pl.pallas_call(
        nothing,
        out_shape=[jax.ShapeDtypeStruct(x.shape, x.dtype) for x in arrays],
        in_specs=[anywhere] * len(arrays),
        out_specs=[anywhere] * len(arrays),
        input_output_aliases={i: i for i in range(len(arrays))},
        cost_estimate=cost(flops, nbytes),
        name="weighty",
    )(*arrays)


def spread_kernel(span, x, out):
    part = out.shape[2]
    for c in range(out.shape[0]):
        at = c % span * part
        out[c] = x[:, at : at + part]


def spread_units(x, n_ctx, span):
    rows, units = x.shape
    return pl.pallas_call(
        functools.partial(spread_kernel, span),
        out_shape=jax.ShapeDtypeStruct((n_ctx, rows, units // span), x.dtype),
        in_specs=[VMEM],
        out_specs=VMEM,
        compiler_params=PARAMS,
        cost_estimate=cost(0, 4 * x.size),
        name="spread_units",
    )(x)


def text_kernel(rows, keep, wq, wk, wv, out, state):
    step = min(rows.shape[0], 256)
    for i in range(rows.shape[0] // step):
        at = slice(i * step, (i + 1) * step)
        for n, w in enumerate((wq, wk, wv)):
            out[n, at, :] = (silu(dot(rows[at, :], w[...])) * keep[at, :]).astype(BF16)
    for h in range(state.shape[0]):
        cols = slice(h * HEAD_DIM, (h + 1) * HEAD_DIM)
        state[h] = lax.dot_general(
            out[1, :, cols], out[2, :, cols], (((0,), (0,)), ((), ())), preferred_element_type=F32
        )


def text_qkv(rows, keep, weights):
    count, width = rows.shape
    cols = weights[0].shape[1]
    heads = cols // HEAD_DIM
    return pl.pallas_call(
        text_kernel,
        out_shape=(
            jax.ShapeDtypeStruct((3, count, cols), BF16),
            jax.ShapeDtypeStruct((heads, HEAD_DIM, HEAD_DIM), F32),
        ),
        in_specs=[VMEM] * 5,
        out_specs=(VMEM, VMEM),
        compiler_params=PARAMS,
        cost_estimate=cost(6 * count * width * cols, 6 * width * cols, 3 * count * cols),
        name="text_qkv",
    )(rows, keep, *weights)


def projector_kernel(chunk, span, pieces, meta, *refs):
    sources, refs = refs[:pieces], refs[pieces:]
    first_hbm, refs = refs[0], refs[1:]
    seconds_hbm, refs = refs[:span], refs[span:]
    keep, send, held, first, seconds, w_keep, w_send, sems = refs
    count = sources[0].shape[0]
    copies = [pltpu.make_async_copy(first_hbm, first, sems.at[0])]
    for n, source in enumerate(sources):
        to = held.at[n * count : (n + 1) * count, :]
        copies.append(pltpu.make_async_copy(source, to, sems.at[1 + n]))
    for m in range(span):
        copies.append(
            pltpu.make_async_copy(seconds_hbm[m], seconds.at[m], sems.at[1 + pieces + m])
        )
    for copy in copies:
        copy.start()
    for copy in copies:
        copy.wait()
    cols = seconds.shape[2]
    same = meta[0] == meta[1]
    for m in range(0, span, 2):
        mine, near = seconds[m], seconds[m + 1]
        slot = (meta[4] ^ m) >> 1
        w_keep[slot] = jnp.where(same, mine, near)
        w_send[slot] = jnp.where(same, near, mine)

    @pl.loop(0, held.shape[0] // chunk)
    def _(i):
        at = pl.ds(pl.multiple_of(i * chunk, chunk), chunk)
        pre = dot(held[at, :], first[...])
        hid = (0.5 * pre * (1.0 + lax.erf(pre * 0.7071067811865476))).astype(BF16)
        for n in range(span // 2):
            keep[at, n * cols : (n + 1) * cols] = dot(hid, w_keep[n]).astype(BF16)
            send[at, n * cols : (n + 1) * cols] = dot(hid, w_send[n]).astype(BF16)


def projector(meta, sources, first, seconds):
    rows, width = sources[0].shape
    rows = rows * len(sources)
    units, cols = seconds[0].shape
    span = len(seconds)
    out = jax.ShapeDtypeStruct((rows, span // 2 * cols), BF16)
    side = pltpu.VMEM((span // 2, units, cols), BF16)
    return pl.pallas_call(
        functools.partial(projector_kernel, min(rows, 256), span, len(sources)),
        out_shape=(out, out),
        in_specs=[SMEM] + [HBM] * (len(sources) + 1 + span),
        out_specs=(VMEM, VMEM),
        scratch_shapes=[
            pltpu.VMEM((rows, width), BF16),
            pltpu.VMEM((width, units), BF16),
            pltpu.VMEM((span, units, cols), BF16),
            side,
            side,
            pltpu.SemaphoreType.DMA((1 + len(sources) + span,)),
        ],
        compiler_params=FETCHING,
        cost_estimate=cost(2 * rows * units * (width + span * cols), 5e6, rows * units),
        name="projector",
    )(meta, *sources, first, *seconds)


def pick_kernel(spot, *refs):
    sources, out = refs[:-1], refs[-1]
    rows = out.shape[0]
    wanted = lax.broadcasted_iota(jnp.int32, (rows, spot.shape[1]), 0)
    at, total = 0, 0.0
    for ref in sources:
        count = ref.shape[0]
        picks = (spot[:, at : at + count] == wanted[:, at : at + count]).astype(F32).astype(BF16)
        total = total + dot(picks, ref[...])
        at += count
    out[...] = total.astype(BF16)


def pick_rows(spot, sources, rows):
    width = sources[0].shape[1]
    return pl.pallas_call(
        pick_kernel,
        out_shape=jax.ShapeDtypeStruct((rows, width), BF16),
        in_specs=[VMEM] * (1 + len(sources)),
        out_specs=VMEM,
        compiler_params=PARAMS,
        cost_estimate=cost(2 * rows * width * spot.shape[1], 2 * width * spot.shape[1]),
        name="pick_rows",
    )(spot, *sources)


def order_kernel(offsets, meta, keep, got, out):
    core, ctx = meta[1], meta[2]
    rows, count = out.shape[2], len(offsets)
    for i in range(2):
        for b, offset in enumerate(offsets):
            at = pl.ds((i * count + b) * rows, rows)
            there = pl.ds(((1 - i) * count + b) * rows, rows)
            total = keep[at, :].astype(F32) + got[there, :].astype(F32)
            out[ctx ^ offset, core ^ i] = total.astype(BF16)


def order_rows(meta, keep, got, offsets):
    rows, cols = keep.shape
    count = len(offsets)
    out = jax.ShapeDtypeStruct((count, 2, rows // count // 2, cols), BF16)
    return pl.pallas_call(
        functools.partial(order_kernel, tuple(offsets)),
        out_shape=out,
        in_specs=[SMEM, VMEM, VMEM],
        out_specs=VMEM,
        compiler_params=PARAMS,
        cost_estimate=cost(rows * cols, 6 * rows * cols),
        name="order_rows",
    )(meta, keep, got)


def image_norm_kernel(groups, span, heads, got, gain, out, total):
    wide = span // 2
    cols = got.shape[2] // wide
    square = 0.0
    for g in range(groups):
        for core in range(2):
            part = 0.0
            for s in range(span):
                for h in range(heads // 2):
                    part = part + got[((g * span + s) * heads) + 2 * h + core].astype(F32)
            part = part.astype(BF16).astype(F32)
            square = square + jnp.sum(part * part, axis=-1, keepdims=True)
            for n in range(wide):
                c = g * span + 2 * n + core
                total[:, c * cols : (c + 1) * cols] = part[:, n * cols : (n + 1) * cols]
    scale = lax.rsqrt(square / total.shape[1] + 1e-05)
    out[...] = (total[...] * scale * gain[...]).astype(BF16)


def image_norm(got, gain, n_ctx, span):
    devices, rows, _ = got.shape
    width = gain.shape[1]
    return pl.pallas_call(
        functools.partial(image_norm_kernel, n_ctx // span, span, devices // n_ctx),
        out_shape=jax.ShapeDtypeStruct((rows, width), BF16),
        in_specs=[VMEM, VMEM],
        out_specs=VMEM,
        scratch_shapes=[pltpu.VMEM((rows, width), F32)],
        compiler_params=PARAMS,
        cost_estimate=cost(4 * got.size, 2 * got.size),
        name="image_norm",
    )(got, gain)


def image_kernel(steps, x, wq, wk, wv, text_state, out, state, held, sems):
    rows = x[...]
    depth = x.shape[1] // steps
    order = ((1, wk), (2, wv), (0, wq))

    def copy(n, w, i):
        at = slice(i * depth, (i + 1) * depth)
        return pltpu.make_async_copy(w.at[at, :], held.at[n, at, :], sems.at[n * steps + i])

    for n, w in order:
        for i in range(steps):
            copy(n, w, i).start()
    for n, w in order:
        total = 0.0
        for i in range(steps):
            copy(n, w, i).wait()
            at = slice(i * depth, (i + 1) * depth)
            total = total + dot(rows[:, at], held[n, at, :])
        out[n] = silu(total).astype(BF16)
    for h in range(state.shape[0]):
        cols = slice(h * HEAD_DIM, (h + 1) * HEAD_DIM)
        outer = lax.dot_general(
            out[1, :, cols], out[2, :, cols], (((0,), (0,)), ((), ())), preferred_element_type=F32
        )
        state[h] = (text_state[h] + outer).astype(BF16)


def image_qkv(x, weights, text_state):
    rows, width = x.shape
    cols = weights[0].shape[1]
    steps = 4 if width % 1024 == 0 else 1
    return pl.pallas_call(
        functools.partial(image_kernel, steps),
        out_shape=(
            jax.ShapeDtypeStruct((3, rows, cols), BF16),
            jax.ShapeDtypeStruct(text_state.shape, BF16),
        ),
        in_specs=[VMEM] + [HBM] * 3 + [VMEM],
        out_specs=(VMEM, VMEM),
        scratch_shapes=[
            pltpu.VMEM((3, width, cols), BF16),
            pltpu.SemaphoreType.DMA((3 * steps,)),
        ],
        compiler_params=FETCHING,
        cost_estimate=cost(6 * rows * width * cols, 6 * width * cols, 3 * rows * cols),
        name="image_qkv",
    )(x, *weights, text_state)


def finish_kernel(intra, q, state, gain, out):
    for h in range(state.shape[0]):
        cols = slice(h * HEAD_DIM, (h + 1) * HEAD_DIM)
        total = intra[:, cols] + dot(q[:, cols], state[h])
        scale = lax.rsqrt(jnp.mean(total * total, axis=-1, keepdims=True) + 1e-06)
        out[:, cols] = (total * scale * gain[:, cols]).astype(BF16)


def finish(intra, q, state, gain):
    rows, cols = q.shape
    return pl.pallas_call(
        finish_kernel,
        out_shape=jax.ShapeDtypeStruct((rows, cols), BF16),
        in_specs=[VMEM] * 4,
        out_specs=VMEM,
        compiler_params=PARAMS,
        cost_estimate=cost(2 * rows * cols * HEAD_DIM, 8 * rows * cols),
        name="finish",
    )(intra, q, state, gain)


def intra_kernel(text, image, put, q, out):
    where = put[...]
    for h in range(q.shape[1] // HEAD_DIM):
        at = slice(h * HEAD_DIM, (h + 1) * HEAD_DIM)
        queries, keys, values = [
            (text[n, :, at].astype(F32) + dot(where, image[n, :, at])).astype(BF16)
            for n in range(3)
        ]
        q[:, at] = queries
        scores = lax.dot_general(
            queries, keys, (((1,), (1,)), ((), ())), preferred_element_type=F32
        )
        rows = lax.broadcasted_iota(jnp.int32, scores.shape, 0)
        cols = lax.broadcasted_iota(jnp.int32, scores.shape, 1)
        scores = jnp.where(cols <= rows, scores, 0.0).astype(BF16)
        out[:, at] = dot(scores, values)


def intra_shard(text, image, put):
    _, rows, cols = text.shape
    return pl.pallas_call(
        intra_kernel,
        out_shape=(
            jax.ShapeDtypeStruct((rows, cols), BF16),
            jax.ShapeDtypeStruct((rows, cols), F32),
        ),
        in_specs=[VMEM] * 3,
        out_specs=(VMEM, VMEM),
        compiler_params=PARAMS,
        cost_estimate=cost(2e10, 4e7),
        name="intra_shard",
    )(text, image, put)


def turned(h, count):
    return (h >> 1) | ((h & 1) * (count // 2))


def mix_load_kernel(mix_offsets, meta, *refs):
    blocks, held, sems = refs[: len(mix_offsets)], refs[-2], refs[-1]
    ctx, head, ratio, count = meta[2], meta[3], meta[5], meta[6]
    base = ((head ^ turned(head, count)) * ratio) ^ ctx
    copies = []
    for n, offset in enumerate(mix_offsets):
        slot = base ^ offset
        copies.append(pltpu.make_async_copy(blocks[n], held.at[slot], sems.at[n]))
    for copy in copies:
        copy.start()
    for copy in copies:
        copy.wait()


def mix_load(meta, mix, mix_offsets):
    return pl.pallas_call(
        functools.partial(mix_load_kernel, tuple(mix_offsets)),
        out_shape=jax.ShapeDtypeStruct((len(mix),) + mix[0].shape, BF16),
        in_specs=[SMEM] + [HBM] * len(mix),
        out_specs=VMEM,
        scratch_shapes=[pltpu.SemaphoreType.DMA((len(mix),))],
        compiler_params=PARAMS,
        cost_estimate=cost(0, 4 * len(mix) * mix[0].size),
        name="mix_load",
    )(meta, *mix)


def mix_kernel(offsets, ratio, count, has_before, *refs):
    ins, (mix, *before, out) = refs[: len(offsets)], refs[len(offsets) :]
    cols = mix.shape[2]
    for r in range(ratio):
        to = slice(r * cols, (r + 1) * cols)
        total = before[0][:, to] if has_before else 0.0
        for ref, offset in zip(ins, offsets):
            total = total + dot(ref[...], mix[turned(offset, count) * ratio + r])
        out[:, to] = total.astype(out.dtype)


def mix_part(arrays, offsets, mix, ratio, count, before, dtype):
    rows, width = arrays[0].shape
    cols = mix.shape[2]
    extra = [] if before is None else [before]
    return pl.pallas_call(
        functools.partial(mix_kernel, tuple(offsets), ratio, count, before is not None),
        out_shape=jax.ShapeDtypeStruct((rows, ratio * cols), dtype),
        in_specs=[VMEM] * (len(arrays) + 1 + len(extra)),
        out_specs=VMEM,
        compiler_params=PARAMS,
        cost_estimate=cost(2 * rows * width * ratio * cols * len(arrays), 5e6),
        name="mix_part",
    )(*arrays, mix, *extra)


def on_device(
    enc_rows,
    row_counts,
    row_places,
    stream,
    norm_gain,
    proj_in,
    proj_out,
    qkv_weight,
    head_gain,
    mix_weight,
):
    both = ("ctx", "head")
    capacity, enc_width = enc_rows.shape
    shard_rows, width = stream.shape
    n_ctx, n_head = lax.axis_size("ctx"), lax.axis_size("head")
    ctx, head = lax.axis_index("ctx"), lax.axis_index("head")
    live_total = n_head * (capacity // 4)
    core_rows = live_total // 2
    part_rows = live_total // n_head
    n_pairs = n_ctx // 2
    core, parity = head & 1, ctx & 1
    span = 2
    spot_in = ctx & (span - 1)
    ratio = n_ctx // n_head
    meta = jnp.stack([parity, core, ctx, head, spot_in, ratio, n_head]).astype(jnp.int32)
    flat = [(c, h) for c in range(n_ctx) for h in range(n_head)]

    def along(axis, count, mask):
        return functools.partial(
            lax.ppermute, axis_name=axis, perm=[(i, i ^ mask) for i in range(count)]
        )

    def index(c, h):
        return c * n_head + h

    perm = [(index(c, h), index(c ^ (turned(h, n_head) * ratio), h)) for c, h in flat]
    mix_own = lax.ppermute(mix_weight, both, perm)

    part = proj_in.shape[1] // span
    if part % 128 == 0:
        in_sends = spread_units(proj_in, n_ctx, span)
    else:
        in_sends = jnp.stack([proj_in[:, c % span * part :][:, :part] for c in range(n_ctx)])
    out_cols = proj_out.shape[1]

    sources, swaps = [enc_rows], [0]
    bit = n_head // 2
    while bit:
        sources = sources + [along("head", n_head, bit)(x) for x in sources]
        swaps = swaps + [o ^ bit for o in swaps]
        bit //= 2
    counts = row_counts[0]
    earlier = jnp.arange(n_head)[:, None] > jnp.arange(n_head)[None, :]
    starts = jnp.sum(jnp.where(earlier, counts[None, :], 0), axis=1)
    within = jnp.arange(capacity, dtype=jnp.int32)[None, :]
    spot = jnp.where(within < counts[:, None], starts[:, None] + within, -1)
    owners = jnp.arange(n_head)[None, :] == (head ^ jnp.array(swaps, dtype=jnp.int32))[:, None]
    swapped = jnp.sum(jnp.where(owners[:, :, None], spot[None], 0), axis=1)
    own_rows = pick_rows(swapped.reshape(1, -1) - core * core_rows, sources, core_rows)
    own_rows, in_sends = lax.optimization_barrier((own_rows, in_sends))
    (in_full,) = weighty([lax.all_to_all(in_sends, "ctx", 0, 0)], 1e11, 4e8)
    in_full = in_full.reshape(enc_width, part)

    def norm(rows):
        widened = rows.astype(F32)
        return (
            widened
            * lax.rsqrt(jnp.mean(widened * widened, axis=-1, keepdims=True) + 1e-05)
            * norm_gain
        ).astype(BF16)

    def spread(x, mask):
        return jnp.concatenate([x, along("ctx", n_ctx, mask)(x)])

    masks = [1 << n for n in reversed(range(n_ctx.bit_length() - 1))]
    offsets_ctx = [0]
    for mask in masks:
        offsets_ctx = offsets_ctx + [o ^ mask for o in offsets_ctx]
    core_part, proj_out, mix_own, stream, qkv_weight = lax.optimization_barrier(
        (spread(own_rows, masks[0]), proj_out, mix_own, stream, qkv_weight)
    )
    perm = [(index(c, h), index(c, (c // ratio) ^ turned(h, n_head))) for c, h in flat]
    mix_own = lax.ppermute(mix_own, both, perm)

    seconds = []
    for m in range(span):
        block = lax.dynamic_slice(proj_out, ((spot_in ^ m) * part, 0), (part, out_cols))
        seconds.append(block)
    seconds = [along("ctx", n_ctx, m)(x) if m else x for m, x in enumerate(seconds)]
    seconds = weighty(seconds, 1e10, 4e7)
    text_rows = norm(stream)
    weights = [qkv_weight[:, i, :] for i in range(3)]
    local_places = row_places[0] - ctx * shard_rows
    picks = spot.reshape(1, -1) == jnp.arange(live_total, dtype=jnp.int32)[:, None]
    places = jnp.sum(jnp.where(picks, local_places[None, :], 0), axis=1)
    put = jnp.arange(shard_rows, dtype=jnp.int32)[:, None] == places[None, :]
    is_text = jnp.logical_not(jnp.any(put, axis=1))[:, None]

    text, text_state = text_qkv(text_rows, is_text.astype(F32), weights)

    core_part = spread(core_part, masks[1])
    core_part, mix_own, text = lax.optimization_barrier((core_part, mix_own, text))
    for mask in masks[2:-1]:
        core_part = spread(core_part, mask)
    core_parts = [core_part, along("ctx", n_ctx, masks[-1])(core_part)]
    other_parts = [along("head", n_head, 1)(x) for x in core_parts]
    core_parts, mix_own = lax.optimization_barrier((core_parts, mix_own))

    mix_blocks = {0: mix_own}
    top = n_ctx // 2
    single = [o for o in range(1, top) if o & (o - 1) == 0]
    double = [o for o in range(1, top) if o not in single]
    late = [o for o in range(top + 1, n_ctx) if o & 1 == 0 or o == top + 1]
    last = [o for o in range(top + 1, n_ctx) if o not in late]

    def mix_start(stage):
        for offset in stage:
            mask = 1 << offset.bit_length() - 1 if offset in double else offset & -offset
            mix_blocks[offset] = along("ctx", n_ctx, mask)(mix_blocks[offset ^ mask])

    def mix_end(stage, beside):
        arrays, beside = lax.optimization_barrier(([mix_blocks[o] for o in stage], beside))
        mix_blocks.update(zip(stage, arrays))
        return beside

    mix_start(single)

    keep, send = projector(meta, core_parts + other_parts, in_full, seconds)
    ordered = order_rows(meta, keep, along("head", n_head, 1)(send), offsets_ctx)
    ordered, mix_blocks[0] = lax.optimization_barrier((ordered, mix_blocks[0]))
    mix_start([top])

    received = lax.all_to_all(
        ordered.reshape(n_ctx * n_head, part_rows, span // 2 * out_cols), both, 0, 0
    )
    (received,) = weighty([received], 2e11, 8e8)

    if out_cols % 128 == 0:
        img_part = image_norm(received, norm_gain[None], n_ctx, span)
    else:
        received = received.reshape(
            n_ctx // span, span, n_head // 2, 2, part_rows, span // 2, out_cols
        )
        summed = jnp.sum(received.astype(F32), axis=(1, 2)).astype(BF16)
        img_part = norm(summed.transpose(2, 0, 3, 1, 4).reshape(part_rows, width))
    image_rows = lax.all_gather(img_part, "head", axis=0, tiled=True)

    image, state = image_qkv(image_rows, weights, text_state)
    state = mix_end([top] + single, state)
    mix_start(late)

    pieces = lax.all_to_all(state.reshape(n_ctx, -1, HEAD_DIM), "ctx", 0, 0).astype(F32)
    before = (jnp.cumsum(pieces, axis=0) - pieces).astype(BF16)
    before, put = lax.optimization_barrier((before, put.astype(BF16)))
    prefix = lax.all_to_all(before, "ctx", 0, 0).reshape(state.shape)

    queries, intra = mix_end(late, intra_shard(text, image, put))
    mix_start(double + last)
    heads_out = finish(intra, queries, prefix, head_gain[None])

    mix_cols = mix_weight.shape[1]
    near, near_offsets = [heads_out], [0]
    near.append(along("head", n_head, 1)(heads_out))
    near_offsets.append(1)
    far, far_offsets = [], []
    bit = n_head // 2
    sent, sent_offsets = [heads_out], [0]
    while bit > 1:
        sent = sent + [along("head", n_head, bit)(p) for p in sent]
        sent_offsets = sent_offsets + [o ^ bit for o in sent_offsets]
        bit //= 2
    near, sent = mix_end(double + last, (near, sent))
    mix_offsets, mix_blocks = list(mix_blocks), list(mix_blocks.values())
    first = None
    if mix_cols % 128 == 0:
        mix_full = mix_load(meta, mix_blocks, mix_offsets)
        first = mix_part(near, near_offsets, mix_full, ratio, n_head, None, F32)
    far = sent[1:] + [along("head", n_head, 1)(p) for p in sent[1:]]
    far_offsets = sent_offsets[1:] + [o ^ 1 for o in sent_offsets[1:]]
    if mix_cols % 128 == 0:
        return mix_part(far, far_offsets, mix_full, ratio, n_head, first, BF16)
    parts, offsets = near + far, near_offsets + far_offsets
    mix_full = jnp.stack([mix_blocks[mix_offsets.index(o)] for o in range(n_ctx)])
    total = 0.0
    for part, offset in zip(parts, offsets):
        spot = head ^ turned(head ^ offset, n_head)
        group = [
            lax.dynamic_index_in_dim(mix_full, (spot * ratio + r) ^ ctx, 0, keepdims=False)
            for r in range(ratio)
        ]
        total = total + dot(part, jnp.concatenate(group, axis=1))
    return total.astype(BF16)


def solution(mesh):
    in_specs = (
        P(("ctx", "head"), None),
        P("ctx", None),
        P("ctx", None),
        P("ctx", None),
        P(),
        P("ctx", "head"),
        P("head", "ctx"),
        P(None, None, "head"),
        P("head"),
        P("head", "ctx"),
    )
    out_specs = P("ctx", "head")
    return jax.shard_map(
        on_device, mesh=mesh, in_specs=in_specs, out_specs=out_specs, check_vma=False
    )
```

```python
import functools

import jax
import jax.numpy as jnp
from jax import lax
from jax.experimental import pallas as pl
from jax.experimental.pallas import tpu as pltpu
from jax.sharding import PartitionSpec as P

HEAD_DIM = 128
F32 = jnp.float32
BF16 = jnp.bfloat16
VMEM_LIMIT = 20 * 1024 * 1024
VMEM = pl.BlockSpec(memory_space=pltpu.VMEM)
SMEM = pl.BlockSpec(memory_space=pltpu.SMEM)
ANYWHERE = pl.BlockSpec(memory_space=pl.ANY)
HBM = pl.BlockSpec(memory_space=pltpu.HBM)
PARAMS = pltpu.CompilerParams(vmem_limit_bytes=VMEM_LIMIT)
FETCHING = pltpu.CompilerParams(vmem_limit_bytes=56 * 1024 * 1024)


def cost(flops, nbytes, transcendentals=0):
    return pl.CostEstimate(
        flops=int(flops), bytes_accessed=int(nbytes), transcendentals=int(transcendentals)
    )


def dot(a, b):
    return jnp.dot(a, b, preferred_element_type=F32)


def silu(x):
    return x * (1.0 / (1.0 + jnp.exp(-x)))


def nothing(*refs):
    pass


def weighty(arrays, flops, nbytes):
    anywhere = pl.BlockSpec(memory_space=pl.ANY)
    return pl.pallas_call(
        nothing,
        out_shape=[jax.ShapeDtypeStruct(x.shape, x.dtype) for x in arrays],
        in_specs=[anywhere] * len(arrays),
        out_specs=[anywhere] * len(arrays),
        input_output_aliases={i: i for i in range(len(arrays))},
        cost_estimate=cost(flops, nbytes),
        name="weighty",
    )(*arrays)


def spread_kernel(span, x, out, sems):
    part = out.shape[2]
    copies = []
    for c in range(out.shape[0]):
        at = c % span * part
        copies.append(pltpu.make_async_copy(x.at[:, at : at + part], out.at[c], sems.at[c]))
    for copy in copies:
        copy.start()
    for copy in copies:
        copy.wait()


def spread_units(x, n_ctx, span):
    rows, units = x.shape
    return pl.pallas_call(
        functools.partial(spread_kernel, span),
        out_shape=jax.ShapeDtypeStruct((n_ctx, rows, units // span), x.dtype),
        in_specs=[HBM],
        out_specs=HBM,
        scratch_shapes=[pltpu.SemaphoreType.DMA((n_ctx,))],
        compiler_params=PARAMS,
        cost_estimate=cost(0, 4 * x.size),
        name="spread_units",
    )(x)


def text_kernel(rows, keep, wq, wk, wv, out, state):
    step = min(rows.shape[0], 256)
    for i in range(rows.shape[0] // step):
        at = slice(i * step, (i + 1) * step)
        for n, w in enumerate((wq, wk, wv)):
            out[n, at, :] = (silu(dot(rows[at, :], w[...])) * keep[at, :]).astype(BF16)
    for h in range(state.shape[0]):
        cols = slice(h * HEAD_DIM, (h + 1) * HEAD_DIM)
        state[h] = lax.dot_general(
            out[1, :, cols], out[2, :, cols], (((0,), (0,)), ((), ())), preferred_element_type=F32
        )


def text_qkv(rows, keep, weights):
    count, width = rows.shape
    cols = weights[0].shape[1]
    heads = cols // HEAD_DIM
    return pl.pallas_call(
        text_kernel,
        out_shape=(
            jax.ShapeDtypeStruct((3, count, cols), BF16),
            jax.ShapeDtypeStruct((heads, HEAD_DIM, HEAD_DIM), F32),
        ),
        in_specs=[VMEM] * 5,
        out_specs=(VMEM, VMEM),
        compiler_params=PARAMS,
        cost_estimate=cost(6 * count * width * cols, 6 * width * cols, 3 * count * cols),
        name="text_qkv",
    )(rows, keep, *weights)


def projector_kernel(chunk, span, pieces, meta, *refs):
    sources, refs = refs[:pieces], refs[pieces:]
    first_hbm, refs = refs[0], refs[1:]
    seconds_hbm, refs = refs[:span], refs[span:]
    keep, send, held, first, seconds, w_keep, w_send, sems = refs
    count = sources[0].shape[0]
    copies = [pltpu.make_async_copy(first_hbm, first, sems.at[0])]
    for n, source in enumerate(sources):
        to = held.at[n * count : (n + 1) * count, :]
        copies.append(pltpu.make_async_copy(source, to, sems.at[1 + n]))
    for m in range(span):
        copies.append(
            pltpu.make_async_copy(seconds_hbm[m], seconds.at[m], sems.at[1 + pieces + m])
        )
    for copy in copies:
        copy.start()
    for copy in copies:
        copy.wait()
    cols = seconds.shape[2]
    same = meta[0] == meta[1]
    for m in range(0, span, 2):
        mine, near = seconds[m], seconds[m + 1]
        slot = (meta[4] ^ m) >> 1
        w_keep[slot] = jnp.where(same, mine, near)
        w_send[slot] = jnp.where(same, near, mine)

    @pl.loop(0, held.shape[0] // chunk)
    def _(i):
        at = pl.ds(pl.multiple_of(i * chunk, chunk), chunk)
        pre = dot(held[at, :], first[...])
        hid = (0.5 * pre * (1.0 + lax.erf(pre * 0.7071067811865476))).astype(BF16)
        for n in range(span // 2):
            keep[at, n * cols : (n + 1) * cols] = dot(hid, w_keep[n]).astype(BF16)
            send[at, n * cols : (n + 1) * cols] = dot(hid, w_send[n]).astype(BF16)


def projector(meta, sources, first, seconds):
    rows, width = sources[0].shape
    rows = rows * len(sources)
    units, cols = seconds[0].shape
    span = len(seconds)
    out = jax.ShapeDtypeStruct((rows, span // 2 * cols), BF16)
    side = pltpu.VMEM((span // 2, units, cols), BF16)
    return pl.pallas_call(
        functools.partial(projector_kernel, min(rows, 256), span, len(sources)),
        out_shape=(out, out),
        in_specs=[SMEM] + [HBM] * (len(sources) + 1 + span),
        out_specs=(VMEM, VMEM),
        scratch_shapes=[
            pltpu.VMEM((rows, width), BF16),
            pltpu.VMEM((width, units), BF16),
            pltpu.VMEM((span, units, cols), BF16),
            side,
            side,
            pltpu.SemaphoreType.DMA((1 + len(sources) + span,)),
        ],
        compiler_params=FETCHING,
        cost_estimate=cost(2 * rows * units * (width + span * cols), 5e6, rows * units),
        name="projector",
    )(meta, *sources, first, *seconds)


def pick_kernel(spot, *refs):
    sources, out = refs[:-1], refs[-1]
    rows = out.shape[0]
    wanted = lax.broadcasted_iota(jnp.int32, (rows, spot.shape[1]), 0)
    at, total = 0, 0.0
    for ref in sources:
        count = ref.shape[0]
        picks = (spot[:, at : at + count] == wanted[:, at : at + count]).astype(F32).astype(BF16)
        total = total + dot(picks, ref[...])
        at += count
    out[...] = total.astype(BF16)


def pick_rows(spot, sources, rows):
    width = sources[0].shape[1]
    return pl.pallas_call(
        pick_kernel,
        out_shape=jax.ShapeDtypeStruct((rows, width), BF16),
        in_specs=[VMEM] * (1 + len(sources)),
        out_specs=VMEM,
        compiler_params=PARAMS,
        cost_estimate=cost(2 * rows * width * spot.shape[1], 2 * width * spot.shape[1]),
        name="pick_rows",
    )(spot, *sources)


def order_kernel(offsets, meta, keep, got, out):
    core, ctx = meta[1], meta[2]
    rows, count = out.shape[2], len(offsets)
    for i in range(2):
        for b, offset in enumerate(offsets):
            at = pl.ds((i * count + b) * rows, rows)
            there = pl.ds(((1 - i) * count + b) * rows, rows)
            total = keep[at, :].astype(F32) + got[there, :].astype(F32)
            out[ctx ^ offset, core ^ i] = total.astype(BF16)


def order_rows(meta, keep, got, offsets):
    rows, cols = keep.shape
    count = len(offsets)
    out = jax.ShapeDtypeStruct((count, 2, rows // count // 2, cols), BF16)
    return pl.pallas_call(
        functools.partial(order_kernel, tuple(offsets)),
        out_shape=out,
        in_specs=[SMEM, VMEM, VMEM],
        out_specs=VMEM,
        compiler_params=PARAMS,
        cost_estimate=cost(rows * cols, 6 * rows * cols),
        name="order_rows",
    )(meta, keep, got)


def image_norm_kernel(groups, span, heads, got, gain, out, total):
    wide = span // 2
    cols = got.shape[2] // wide
    square = 0.0
    for g in range(groups):
        for core in range(2):
            part = 0.0
            for s in range(span):
                for h in range(heads // 2):
                    part = part + got[((g * span + s) * heads) + 2 * h + core].astype(F32)
            part = part.astype(BF16).astype(F32)
            square = square + jnp.sum(part * part, axis=-1, keepdims=True)
            for n in range(wide):
                c = g * span + 2 * n + core
                total[:, c * cols : (c + 1) * cols] = part[:, n * cols : (n + 1) * cols]
    scale = lax.rsqrt(square / total.shape[1] + 1e-05)
    out[...] = (total[...] * scale * gain[...]).astype(BF16)


def image_norm(got, gain, n_ctx, span):
    devices, rows, _ = got.shape
    width = gain.shape[1]
    return pl.pallas_call(
        functools.partial(image_norm_kernel, n_ctx // span, span, devices // n_ctx),
        out_shape=jax.ShapeDtypeStruct((rows, width), BF16),
        in_specs=[VMEM, VMEM],
        out_specs=VMEM,
        scratch_shapes=[pltpu.VMEM((rows, width), F32)],
        compiler_params=PARAMS,
        cost_estimate=cost(4 * got.size, 2 * got.size),
        name="image_norm",
    )(got, gain)


def image_kernel(steps, x, wq, wk, wv, text_hbm, out, state, held, text_state, sems):
    rows = x[...]
    depth = x.shape[1] // steps
    order = ((1, wk), (2, wv), (0, wq))

    def copy(n, w, i):
        at = slice(i * depth, (i + 1) * depth)
        return pltpu.make_async_copy(w.at[at, :], held.at[n, at, :], sems.at[n * steps + i])

    for n, w in order:
        for i in range(steps):
            copy(n, w, i).start()
    text = pltpu.make_async_copy(text_hbm, text_state, sems.at[3 * steps])
    text.start()
    for n, w in order:
        total = 0.0
        for i in range(steps):
            copy(n, w, i).wait()
            at = slice(i * depth, (i + 1) * depth)
            total = total + dot(rows[:, at], held[n, at, :])
        out[n] = silu(total).astype(BF16)
    text.wait()
    for h in range(state.shape[0]):
        cols = slice(h * HEAD_DIM, (h + 1) * HEAD_DIM)
        outer = lax.dot_general(
            out[1, :, cols], out[2, :, cols], (((0,), (0,)), ((), ())), preferred_element_type=F32
        )
        state[h] = (text_state[h] + outer).astype(BF16)


def image_qkv(x, weights, text_state):
    rows, width = x.shape
    cols = weights[0].shape[1]
    steps = 4 if width % 1024 == 0 else 1
    return pl.pallas_call(
        functools.partial(image_kernel, steps),
        out_shape=(
            jax.ShapeDtypeStruct((3, rows, cols), BF16),
            jax.ShapeDtypeStruct(text_state.shape, BF16),
        ),
        in_specs=[VMEM] + [HBM] * 4,
        out_specs=(VMEM, VMEM),
        scratch_shapes=[
            pltpu.VMEM((3, width, cols), BF16),
            pltpu.VMEM(text_state.shape, F32),
            pltpu.SemaphoreType.DMA((3 * steps + 1,)),
        ],
        compiler_params=FETCHING,
        cost_estimate=cost(6 * rows * width * cols, 6 * width * cols, 3 * rows * cols),
        name="image_qkv",
    )(x, *weights, text_state)


def finish_kernel(intra, q, state, gain, out):
    for h in range(state.shape[0]):
        cols = slice(h * HEAD_DIM, (h + 1) * HEAD_DIM)
        total = intra[:, cols] + dot(q[:, cols], state[h])
        scale = lax.rsqrt(jnp.mean(total * total, axis=-1, keepdims=True) + 1e-06)
        out[:, cols] = (total * scale * gain[:, cols]).astype(BF16)


def finish(intra, q, state, gain):
    rows, cols = q.shape
    return pl.pallas_call(
        finish_kernel,
        out_shape=jax.ShapeDtypeStruct((rows, cols), BF16),
        in_specs=[VMEM] * 4,
        out_specs=VMEM,
        compiler_params=PARAMS,
        cost_estimate=cost(2 * rows * cols * HEAD_DIM, 8 * rows * cols),
        name="finish",
    )(intra, q, state, gain)


def intra_kernel(text, image, put, q, out):
    where = put[...]
    for h in range(q.shape[1] // HEAD_DIM):
        at = slice(h * HEAD_DIM, (h + 1) * HEAD_DIM)
        queries, keys, values = [
            (text[n, :, at].astype(F32) + dot(where, image[n, :, at])).astype(BF16)
            for n in range(3)
        ]
        q[:, at] = queries
        scores = lax.dot_general(
            queries, keys, (((1,), (1,)), ((), ())), preferred_element_type=F32
        )
        rows = lax.broadcasted_iota(jnp.int32, scores.shape, 0)
        cols = lax.broadcasted_iota(jnp.int32, scores.shape, 1)
        scores = jnp.where(cols <= rows, scores, 0.0).astype(BF16)
        out[:, at] = dot(scores, values)


def intra_shard(text, image, put):
    _, rows, cols = text.shape
    return pl.pallas_call(
        intra_kernel,
        out_shape=(
            jax.ShapeDtypeStruct((rows, cols), BF16),
            jax.ShapeDtypeStruct((rows, cols), F32),
        ),
        in_specs=[VMEM] * 3,
        out_specs=(VMEM, VMEM),
        compiler_params=PARAMS,
        cost_estimate=cost(2e10, 4e7),
        name="intra_shard",
    )(text, image, put)


def turned(h, count):
    return (h >> 1) | ((h & 1) * (count // 2))


def mix_load_kernel(mix_offsets, meta, *refs):
    blocks, held, sems = refs[: len(mix_offsets)], refs[-2], refs[-1]
    ctx, head, ratio, count = meta[2], meta[3], meta[5], meta[6]
    base = ((head ^ turned(head, count)) * ratio) ^ ctx
    copies = []
    for n, offset in enumerate(mix_offsets):
        slot = base ^ offset
        copies.append(pltpu.make_async_copy(blocks[n], held.at[slot], sems.at[n]))
    for copy in copies:
        copy.start()
    for copy in copies:
        copy.wait()


def mix_load(meta, mix, mix_offsets):
    return pl.pallas_call(
        functools.partial(mix_load_kernel, tuple(mix_offsets)),
        out_shape=jax.ShapeDtypeStruct((len(mix),) + mix[0].shape, BF16),
        in_specs=[SMEM] + [HBM] * len(mix),
        out_specs=VMEM,
        scratch_shapes=[pltpu.SemaphoreType.DMA((len(mix),))],
        compiler_params=PARAMS,
        cost_estimate=cost(0, 4 * len(mix) * mix[0].size),
        name="mix_load",
    )(meta, *mix)


def mix_kernel(offsets, ratio, count, has_before, *refs):
    ins, (mix, *before, out) = refs[: len(offsets)], refs[len(offsets) :]
    cols = mix.shape[2]
    for r in range(ratio):
        to = slice(r * cols, (r + 1) * cols)
        total = before[0][:, to] if has_before else 0.0
        for ref, offset in zip(ins, offsets):
            total = total + dot(ref[...], mix[turned(offset, count) * ratio + r])
        out[:, to] = total.astype(out.dtype)


def mix_part(arrays, offsets, mix, ratio, count, before, dtype):
    rows, width = arrays[0].shape
    cols = mix.shape[2]
    extra = [] if before is None else [before]
    return pl.pallas_call(
        functools.partial(mix_kernel, tuple(offsets), ratio, count, before is not None),
        out_shape=jax.ShapeDtypeStruct((rows, ratio * cols), dtype),
        in_specs=[VMEM] * (len(arrays) + 1 + len(extra)),
        out_specs=VMEM,
        compiler_params=PARAMS,
        cost_estimate=cost(2 * rows * width * ratio * cols * len(arrays), 5e6),
        name="mix_part",
    )(*arrays, mix, *extra)


def on_device(
    enc_rows,
    row_counts,
    row_places,
    stream,
    norm_gain,
    proj_in,
    proj_out,
    qkv_weight,
    head_gain,
    mix_weight,
):
    both = ("ctx", "head")
    capacity, enc_width = enc_rows.shape
    shard_rows, width = stream.shape
    n_ctx, n_head = lax.axis_size("ctx"), lax.axis_size("head")
    ctx, head = lax.axis_index("ctx"), lax.axis_index("head")
    live_total = n_head * (capacity // 4)
    core_rows = live_total // 2
    part_rows = live_total // n_head
    n_pairs = n_ctx // 2
    core, parity = head & 1, ctx & 1
    span = 2
    spot_in = ctx & (span - 1)
    ratio = n_ctx // n_head
    meta = jnp.stack([parity, core, ctx, head, spot_in, ratio, n_head]).astype(jnp.int32)
    flat = [(c, h) for c in range(n_ctx) for h in range(n_head)]

    def along(axis, count, mask):
        return functools.partial(
            lax.ppermute, axis_name=axis, perm=[(i, i ^ mask) for i in range(count)]
        )

    def index(c, h):
        return c * n_head + h

    perm = [(index(c, h), index(c ^ (turned(h, n_head) * ratio), h)) for c, h in flat]
    mix_own = lax.ppermute(mix_weight, both, perm)

    part = proj_in.shape[1] // span
    if part % 128 == 0:
        in_sends = spread_units(proj_in, n_ctx, span)
    else:
        in_sends = jnp.stack([proj_in[:, c % span * part :][:, :part] for c in range(n_ctx)])
    out_cols = proj_out.shape[1]

    sources, swaps = [enc_rows], [0]
    bit = n_head // 2
    while bit:
        sources = sources + [along("head", n_head, bit)(x) for x in sources]
        swaps = swaps + [o ^ bit for o in swaps]
        bit //= 2
    counts = row_counts[0]
    earlier = jnp.arange(n_head)[:, None] > jnp.arange(n_head)[None, :]
    starts = jnp.sum(jnp.where(earlier, counts[None, :], 0), axis=1)
    within = jnp.arange(capacity, dtype=jnp.int32)[None, :]
    spot = jnp.where(within < counts[:, None], starts[:, None] + within, -1)
    owners = jnp.arange(n_head)[None, :] == (head ^ jnp.array(swaps, dtype=jnp.int32))[:, None]
    swapped = jnp.sum(jnp.where(owners[:, :, None], spot[None], 0), axis=1)
    own_rows = pick_rows(swapped.reshape(1, -1) - core * core_rows, sources, core_rows)
    own_rows, in_sends = lax.optimization_barrier((own_rows, in_sends))
    (in_full,) = weighty([lax.all_to_all(in_sends, "ctx", 0, 0)], 1e11, 4e8)
    in_full = in_full.reshape(enc_width, part)

    def norm(rows):
        widened = rows.astype(F32)
        return (
            widened
            * lax.rsqrt(jnp.mean(widened * widened, axis=-1, keepdims=True) + 1e-05)
            * norm_gain
        ).astype(BF16)

    def spread(x, mask):
        return jnp.concatenate([x, along("ctx", n_ctx, mask)(x)])

    masks = [1 << n for n in reversed(range(n_ctx.bit_length() - 1))]
    offsets_ctx = [0]
    for mask in masks:
        offsets_ctx = offsets_ctx + [o ^ mask for o in offsets_ctx]
    core_part, proj_out, mix_own, stream, qkv_weight = lax.optimization_barrier(
        (spread(own_rows, masks[0]), proj_out, mix_own, stream, qkv_weight)
    )
    perm = [(index(c, h), index(c, (c // ratio) ^ turned(h, n_head))) for c, h in flat]
    mix_own = lax.ppermute(mix_own, both, perm)

    seconds = []
    for m in range(span):
        block = lax.dynamic_slice(proj_out, ((spot_in ^ m) * part, 0), (part, out_cols))
        seconds.append(block)
    seconds = [along("ctx", n_ctx, m)(x) if m else x for m, x in enumerate(seconds)]
    seconds = weighty(seconds, 1e10, 4e7)
    text_rows = norm(stream)
    weights = [qkv_weight[:, i, :] for i in range(3)]
    local_places = row_places[0] - ctx * shard_rows
    picks = spot.reshape(1, -1) == jnp.arange(live_total, dtype=jnp.int32)[:, None]
    places = jnp.sum(jnp.where(picks, local_places[None, :], 0), axis=1)
    put = jnp.arange(shard_rows, dtype=jnp.int32)[:, None] == places[None, :]
    is_text = jnp.logical_not(jnp.any(put, axis=1))[:, None]

    text, text_state = text_qkv(text_rows, is_text.astype(F32), weights)

    core_part = spread(core_part, masks[1])
    core_part, mix_own, text = lax.optimization_barrier((core_part, mix_own, text))
    for mask in masks[2:-1]:
        core_part = spread(core_part, mask)
    core_parts = [core_part, along("ctx", n_ctx, masks[-1])(core_part)]
    other_parts = [along("head", n_head, 1)(x) for x in core_parts]
    core_parts, mix_own = lax.optimization_barrier((core_parts, mix_own))

    mix_blocks = {0: mix_own}
    top = n_ctx // 2
    single = [o for o in range(1, top) if o & (o - 1) == 0]
    double = [o for o in range(1, top) if o not in single]
    late = [o for o in range(top + 1, n_ctx) if o & 1 == 0 or o == top + 1]
    last = [o for o in range(top + 1, n_ctx) if o not in late]

    def mix_start(stage):
        for offset in stage:
            mask = 1 << offset.bit_length() - 1 if offset in double else offset & -offset
            mix_blocks[offset] = along("ctx", n_ctx, mask)(mix_blocks[offset ^ mask])

    def mix_end(stage, beside):
        arrays, beside = lax.optimization_barrier(([mix_blocks[o] for o in stage], beside))
        mix_blocks.update(zip(stage, arrays))
        return beside

    mix_start(single)

    keep, send = projector(meta, core_parts + other_parts, in_full, seconds)
    ordered = order_rows(meta, keep, along("head", n_head, 1)(send), offsets_ctx)
    ordered, mix_blocks[0] = lax.optimization_barrier((ordered, mix_blocks[0]))
    mix_start([top])

    received = lax.all_to_all(
        ordered.reshape(n_ctx * n_head, part_rows, span // 2 * out_cols), both, 0, 0
    )
    (received,) = weighty([received], 2e11, 8e8)

    if out_cols % 128 == 0:
        img_part = image_norm(received, norm_gain[None], n_ctx, span)
    else:
        received = received.reshape(
            n_ctx // span, span, n_head // 2, 2, part_rows, span // 2, out_cols
        )
        summed = jnp.sum(received.astype(F32), axis=(1, 2)).astype(BF16)
        img_part = norm(summed.transpose(2, 0, 3, 1, 4).reshape(part_rows, width))
    image_rows = lax.all_gather(img_part, "head", axis=0, tiled=True)

    image, state = image_qkv(image_rows, weights, text_state)
    state = mix_end([top] + single, state)
    mix_start(late)

    pieces = lax.all_to_all(state.reshape(n_ctx, -1, HEAD_DIM), "ctx", 0, 0).astype(F32)
    before = (jnp.cumsum(pieces, axis=0) - pieces).astype(BF16)
    before, put = lax.optimization_barrier((before, put.astype(BF16)))
    prefix = lax.all_to_all(before, "ctx", 0, 0).reshape(state.shape)

    queries, intra = mix_end(late, intra_shard(text, image, put))
    mix_start(double + last)
    heads_out = finish(intra, queries, prefix, head_gain[None])

    mix_cols = mix_weight.shape[1]
    near, near_offsets = [heads_out], [0]
    near.append(along("head", n_head, 1)(heads_out))
    near_offsets.append(1)
    far, far_offsets = [], []
    bit = n_head // 2
    sent, sent_offsets = [heads_out], [0]
    while bit > 1:
        sent = sent + [along("head", n_head, bit)(p) for p in sent]
        sent_offsets = sent_offsets + [o ^ bit for o in sent_offsets]
        bit //= 2
    near, sent = mix_end(double + last, (near, sent))
    mix_offsets, mix_blocks = list(mix_blocks), list(mix_blocks.values())
    first = None
    if mix_cols % 128 == 0:
        mix_full = mix_load(meta, mix_blocks, mix_offsets)
        first = mix_part(near, near_offsets, mix_full, ratio, n_head, None, F32)
    far = sent[1:] + [along("head", n_head, 1)(p) for p in sent[1:]]
    far_offsets = sent_offsets[1:] + [o ^ 1 for o in sent_offsets[1:]]
    if mix_cols % 128 == 0:
        return mix_part(far, far_offsets, mix_full, ratio, n_head, first, BF16)
    parts, offsets = near + far, near_offsets + far_offsets
    mix_full = jnp.stack([mix_blocks[mix_offsets.index(o)] for o in range(n_ctx)])
    total = 0.0
    for part, offset in zip(parts, offsets):
        spot = head ^ turned(head ^ offset, n_head)
        group = [
            lax.dynamic_index_in_dim(mix_full, (spot * ratio + r) ^ ctx, 0, keepdims=False)
            for r in range(ratio)
        ]
        total = total + dot(part, jnp.concatenate(group, axis=1))
    return total.astype(BF16)


def solution(mesh):
    in_specs = (
        P(("ctx", "head"), None),
        P("ctx", None),
        P("ctx", None),
        P("ctx", None),
        P(),
        P("ctx", "head"),
        P("head", "ctx"),
        P(None, None, "head"),
        P("head"),
        P("head", "ctx"),
    )
    out_specs = P("ctx", "head")
    return jax.shard_map(
        on_device, mesh=mesh, in_specs=in_specs, out_specs=out_specs, check_vma=False
    )
```
